32 devices in a mesh: req: 16 (over z, x, core), tp: 2 (over y).
Axes of the slice: x: 2, y: 2, z: 4, core: 2. Of those that a mesh axis runs over, the one named last changes fastest.
Arguments:
- queries: bfloat16 [4, 128, 1024], P(None, 'req', 'tp'), may hold values from -6 to 6
- new_kv: bfloat16 [4, 128, 2, 1024], P(None, 'req', None, 'tp'), may hold values from -4 to 4
- residual: bfloat16 [4, 128, 2048], P(None, 'req'), may hold values from -1.1953125 to 1.1953125
- home_cache: bfloat16 [64, 128, 2, 1024], P('req', None, None, 'tp'), may hold values from -6 to 6
- prompt_cache: bfloat16 [64, 128, 2, 1024], P('req', None, None, 'tp'), may hold values from -6 to 6
- home_table: int32 [128, 4], P('req'), may hold values from 0 to 3
- home_len: int32 [128], P('req'), may hold values from 1 to 512, as said below
- parents: int32 [4, 128], P(None, 'req'), may hold values from 0 to 7
- prompt_place: int32 [16], P('req'), may hold values from 0 to 15, as said below
- owned_request: int32 [16], P('req'), may hold values from 0 to 15, as said below
- prompt_len: int32 [16], P('req'), may hold values from 1 to 512, as said below
- out_weight: bfloat16 [1024, 2048], P('tp'), may hold values from -0.1875 to 0.1875
- norm_gain: bfloat16 [2048], replicated, may hold values from 0.099609375 to 1.8984375
- qkv_weight: bfloat16 [2048, 3, 1024], P(None, None, 'tp'), may hold values from -0.03125 to 0.03125
Outputs:
- next_qkv: bfloat16 [4, 128, 3, 1024], P(None, 'req', None, 'tp')
- new_residual: bfloat16 [4, 128, 2048], P(None, 'req')
The draws below stay inside these ranges and needn't reach their ends.
Inputs may be any that keep to these rules, and one draw needn't show every extreme that they name: `home_len`: some beam has all 512 tokens. `prompt_len`: some prompt has all 512 tokens. `prompt_place`: A permutation. Slot j lies on device j. The 1 request of one device have their prompts on 1 different devices, each device holds prompts of 1 request of different devices, and a request's position among its device's requests equals its slot's position j % 1. `owned_request`: the inverse permutation of prompt_place.
All inputs are finite; a program needn't handle non-finite values.
Results may differ from the reference program's by a relative error of at most 0.013.
Values may be sent and summed in bfloat16 or wider, within the bound.
A program may use at most 128 MiB of HBM per device.

```python
import math
import jax
import jax.numpy as jnp
from jax import lax

D = 2048
HEADS = 16
HEAD_DIM = 64
BLOCK = 128
BEAMS = 8
HOME_BLOCKS = 4
PROMPT_BLOCKS = 4
STEPS = 4
REQ_DEV = 1
REQUESTS = 16
BEAMS_DEV = 8
ROWS = 128
POOL_DEV = 4


def cache_blocks(key, salt, block_total):
    first, second = jax.random.split(jax.random.fold_in(key, salt))
    array_shape = (block_total, BLOCK, HEADS * HEAD_DIM)
    key_part = jnp.clip(jax.random.normal(first, array_shape, jnp.float32), -4.0, 4.0)
    value_part = jnp.clip(jax.random.normal(second, array_shape, jnp.float32), -4.0, 4.0)
    return jnp.stack([key_part, value_part], axis=2).astype(jnp.bfloat16)


def draw_home_cache(key, part):
    return cache_blocks(key, 1, POOL_DEV * REQUESTS // REQ_DEV)


def draw_prompt_cache(key, part):
    return cache_blocks(key, 2, PROMPT_BLOCKS * REQUESTS)


def draw_queries(key, part):
    array_shape = (STEPS, BEAMS * REQUESTS, HEADS * HEAD_DIM)
    first = jax.random.fold_in(key, 3)
    result = jnp.clip(jax.random.normal(first, array_shape, jnp.float32), -4.0, 4.0)
    return result.astype(jnp.bfloat16)


def draw_home_len(key, part):
    most_tokens = HOME_BLOCKS * BLOCK
    drawn = jax.random.randint(jax.random.fold_in(key, 5), (BEAMS * REQUESTS,), 1, most_tokens + 1)
    return drawn.at[0].set(most_tokens).astype(jnp.int32)


def draw_prompt_len(key, part):
    most_tokens = PROMPT_BLOCKS * BLOCK
    drawn = jax.random.randint(jax.random.fold_in(key, 6), (REQUESTS,), 1, most_tokens + 1)
    return drawn.at[REQUESTS - 1].set(most_tokens).astype(jnp.int32)


def placement(key):
    device_total = REQUESTS // REQ_DEV
    salted = jax.random.fold_in(key, 4242)
    owner_perm = jax.random.permutation(jax.random.fold_in(salted, 1), device_total)
    home_perm = jax.random.permutation(jax.random.fold_in(salted, 2), device_total)
    offsets = jax.random.permutation(jax.random.fold_in(salted, 3), device_total)[:REQ_DEV]
    request_ids = jnp.arange(REQUESTS, dtype=jnp.int32)
    home_device = request_ids // REQ_DEV
    local_index = request_ids % REQ_DEV
    owner_slot = owner_perm[(home_perm[home_device] + offsets[local_index]) % device_total]
    placed = (owner_slot * REQ_DEV + local_index).astype(jnp.int32)
    holders = jnp.zeros((REQUESTS,), jnp.int32).at[placed].set(request_ids)
    return (placed, holders)


def draw_prompt_place(key, part):
    return placement(key)[0]


def draw_owned_request(key, part):
    return placement(key)[1]


def plant(values, rng, low, top_value):
    dims = values.shape
    index_at = [jax.random.randint(jax.random.fold_in(rng, axis), (), 0, dims[axis]) for axis in range(len(dims))]
    values = values.at[tuple(index_at)].set(low)
    longest = dims.index(max(dims))
    index_at[longest] = (index_at[longest] + 1) % dims[longest]
    return values.at[tuple(index_at)].set(top_value)


def levels(own_key, extent, pieces, smallest, largest):
    def one(position, parts):
        draws = jax.random.uniform(jax.random.fold_in(jax.random.fold_in(own_key, 6), position), (parts,), jnp.float32, smallest / len(pieces), largest / len(pieces))
        return jnp.repeat(jnp.exp(draws), extent[position] // parts).reshape((-1,) + (1,) * (len(extent) - position - 1))

    factor_of = one(*pieces[0])
    for cut in pieces[1:]:
        factor_of = factor_of * one(*cut)
    return factor_of


def scatter_about(rng, shape, width, most, pieces=(), held_as=jnp.bfloat16):
    values = width * jax.random.normal(rng, shape, jnp.float32)
    if pieces:
        values = values * levels(rng, shape, pieces, -0.22, 0.18)
    return jnp.clip(values, -most, most).astype(held_as)


def setup_inputs(seed: int = 0) -> dict:
    splits = jax.random.split(jax.random.key(seed), 15)
    return {
        "queries": draw_queries(jax.random.fold_in(splits[14], 71), 0),
        "new_kv": scatter_about(splits[1], (STEPS, ROWS, 2, HEADS * HEAD_DIM), 1.0, 4.0, ((1, 16), (3, 2))),
        "residual": scatter_about(splits[2], (STEPS, ROWS, D), 0.3, 1.1953125, ((1, 16),)),
        "home_cache": draw_home_cache(jax.random.fold_in(splits[14], 71), 0),
        "prompt_cache": draw_prompt_cache(jax.random.fold_in(splits[14], 71), 0),
        "home_table": plant(jax.random.randint(splits[5], (ROWS, HOME_BLOCKS), 0, POOL_DEV), jax.random.fold_in(splits[5], 1), 0, POOL_DEV - 1).astype(jnp.int32),
        "home_len": draw_home_len(jax.random.fold_in(splits[14], 71), 0),
        "parents": plant(jax.random.randint(splits[7], (STEPS, ROWS), 0, BEAMS), jax.random.fold_in(splits[7], 1), 0, BEAMS - 1).astype(jnp.int32),
        "prompt_place": draw_prompt_place(jax.random.fold_in(splits[14], 71), 0),
        "owned_request": draw_owned_request(jax.random.fold_in(splits[14], 71), 0),
        "prompt_len": draw_prompt_len(jax.random.fold_in(splits[14], 71), 0),
        "out_weight": scatter_about(splits[11], (HEADS * HEAD_DIM, D), (HEADS * HEAD_DIM) ** -0.5, 0.1875, ((0, 2),)),
        "norm_gain": jnp.clip(1.0 + 0.18 * jax.random.normal(splits[12], (D,), jnp.float32), 0.099609375, 1.8984375).astype(jnp.bfloat16),
        "qkv_weight": scatter_about(splits[13], (D, 3, HEADS * HEAD_DIM), (16 * D) ** -0.5, 0.03125, ((2, 2),)),
    }


NEG_FILL = -1e+30
NORM_EPS = 1e-05

def reference(queries, new_kv, residual, home_cache, prompt_cache, home_table, home_len, parents, prompt_place, owned_request, prompt_len, out_weight, norm_gain, qkv_weight):
    lane_width = HEADS * HEAD_DIM
    row_count = queries.shape[1]
    request_count = row_count // BEAMS
    score_scale = 1.0 / math.sqrt(HEAD_DIM)
    row_index = jnp.arange(row_count, dtype=jnp.int32)
    request_base = row_index // BEAMS * BEAMS
    device_of_row = row_index // BEAMS_DEV
    tables = home_table + (device_of_row * POOL_DEV)[:, None]
    first_parent = request_base + parents[0]
    tables = tables[first_parent]
    lengths = home_len[first_parent]
    window = jnp.zeros((row_count, STEPS, 2, lane_width), jnp.bfloat16)
    prompt_tokens = PROMPT_BLOCKS * BLOCK
    home_tokens = HOME_BLOCKS * BLOCK
    prompts = prompt_cache.reshape(REQUESTS, prompt_tokens, 2, lane_width)
    live_prompt = prompt_len[prompt_place]
    prompt_asker = owned_request[prompt_place]
    prompt_pos = jnp.arange(prompt_tokens, dtype=jnp.int32)
    home_pos = jnp.arange(home_tokens, dtype=jnp.int32)
    window_pos = jnp.arange(STEPS, dtype=jnp.int32)
    gain_row = norm_gain.astype(jnp.float32)
    weight_flat = qkv_weight.reshape(D, 3 * lane_width)
    qkv_list = []
    residual_list = []
    for step_index in range(STEPS):
        if step_index > 0:
            window = window.at[:, step_index - 1].set(new_kv[step_index - 1])
            chosen = request_base + parents[step_index]
            window = window[chosen]
            tables = tables[chosen]
            lengths = lengths[chosen]
        step_queries = queries[step_index].reshape(request_count, BEAMS, lane_width)

        def attend(item_parts):
            query_rows, asker_rows, table_rows, length_rows, window_rows, own_rows, prompt_slot, prompt_live = item_parts
            query_heads = query_rows.reshape(BEAMS, HEADS, HEAD_DIM).astype(jnp.float32)
            asker_heads = asker_rows.reshape(BEAMS, HEADS, HEAD_DIM).astype(jnp.float32)
            prompt_rows = lax.dynamic_index_in_dim(prompts, prompt_slot, 0, keepdims=False)
            prompt_rows = prompt_rows.reshape(prompt_tokens, 2, HEADS, HEAD_DIM).astype(jnp.float32)
            home_rows = home_cache[table_rows].reshape(BEAMS, home_tokens, 2, HEADS, HEAD_DIM).astype(jnp.float32)
            window_heads = window_rows.reshape(BEAMS, STEPS, 2, HEADS, HEAD_DIM).astype(jnp.float32)
            own_heads = own_rows.reshape(BEAMS, 2, HEADS, HEAD_DIM).astype(jnp.float32)
            prompt_scores = jnp.einsum('bhd,thd->bht', asker_heads, prompt_rows[:, 0]) * score_scale
            prompt_scores = jnp.where(prompt_pos < prompt_live, prompt_scores, NEG_FILL)
            home_scores = jnp.einsum('bhd,bthd->bht', query_heads, home_rows[:, :, 0]) * score_scale
            home_scores = jnp.where(home_pos[None, None, :] < length_rows[:, None, None], home_scores, NEG_FILL)
            window_scores = jnp.einsum('bhd,bthd->bht', query_heads, window_heads[:, :, 0]) * score_scale
            window_scores = jnp.where(window_pos < step_index, window_scores, NEG_FILL)
            own_scores = jnp.einsum('bhd,bhd->bh', query_heads, own_heads[:, 0])[:, :, None] * score_scale
            scores = jnp.concatenate([prompt_scores, home_scores, window_scores, own_scores], axis=-1)
            row_top = lax.optimization_barrier(jnp.max(scores, axis=-1, keepdims=True))
            weights = jnp.exp(scores - row_top).astype(jnp.bfloat16)
            weights = lax.optimization_barrier(weights).astype(jnp.float32)
            weight_sum = lax.optimization_barrier(jnp.sum(weights, axis=-1))
            split_one = prompt_tokens
            split_two = prompt_tokens + home_tokens
            numerator = jnp.einsum('bht,thd->bhd', weights[:, :, :split_one], prompt_rows[:, 1])
            numerator = numerator + jnp.einsum('bht,bthd->bhd', weights[:, :, split_one:split_two], home_rows[:, :, 1])
            numerator = numerator + jnp.einsum('bht,bthd->bhd', weights[:, :, split_two:split_two + STEPS], window_heads[:, :, 1])
            numerator = numerator + weights[:, :, -1:] * own_heads[:, 1]
            return (numerator / weight_sum[:, :, None]).astype(jnp.bfloat16).reshape(BEAMS, lane_width)
        attended = lax.map(attend, (step_queries, step_queries[prompt_asker], tables.reshape(request_count, BEAMS, HOME_BLOCKS), lengths.reshape(request_count, BEAMS), window.reshape(request_count, BEAMS, STEPS, 2, lane_width), new_kv[step_index].reshape(request_count, BEAMS, 2, lane_width), prompt_place, live_prompt)).reshape(row_count, lane_width)
        mixed_rows = residual[step_index].astype(jnp.float32) + jnp.dot(attended, out_weight, preferred_element_type=jnp.float32)
        residual_list.append(mixed_rows.astype(jnp.bfloat16))
        mean_square = lax.optimization_barrier(jnp.mean(mixed_rows * mixed_rows, axis=-1, keepdims=True))
        normed = (mixed_rows * lax.rsqrt(mean_square + NORM_EPS) * gain_row).astype(jnp.bfloat16)
        projected = jnp.dot(normed, weight_flat, preferred_element_type=jnp.float32).astype(jnp.bfloat16)
        qkv_list.append(projected.reshape(row_count, 3, lane_width))
    return (jnp.stack(qkv_list), jnp.stack(residual_list))
```

```python
import functools
import math

import jax
import jax.numpy as jnp
from jax import lax
from jax.experimental import pallas as pl
from jax.experimental.pallas import tpu as pltpu
from jax.sharding import PartitionSpec as P

HEAD_DIM = 64
BEAMS = 8
LANES = 128
OUT_CHUNKS = 4

NEG_FILL = -1e30
NORM_EPS = 1e-05


def grid_of(req_size):
    chips = req_size // 2
    outer = 4 if chips % 4 == 0 else 1
    return outer, chips // outer


def spread_heads(q, heads):
    rows, lanes = q.shape
    scaled = q.astype(jnp.float32) * (1.0 / math.sqrt(HEAD_DIM))
    lane_head = lax.broadcasted_iota(jnp.int32, (rows, lanes), 1) // HEAD_DIM
    parts = [jnp.where(lane_head == h, scaled, 0.0) for h in range(heads)]
    return jnp.concatenate(parts, axis=0).astype(jnp.bfloat16)


def dot_t(a, b):
    return lax.dot_general(a, b, (((1,), (1,)), ((), ())), preferred_element_type=jnp.float32)


def own_columns(wide, rows, lanes):
    first = lax.broadcasted_iota(jnp.int32, (rows, LANES), 1) < HEAD_DIM
    tiles = []
    for t in range(lanes // LANES):
        cols = slice(t * LANES, (t + 1) * LANES)
        a = wide[2 * t * rows : (2 * t + 1) * rows, cols]
        b = wide[(2 * t + 1) * rows : (2 * t + 2) * rows, cols]
        tiles.append(jnp.where(first, a, b))
    return tiles[0] if len(tiles) == 1 else jnp.concatenate(tiles, axis=1)


def kernel(
    req_size, tp_size, steps,
    table_ref, len_ref, parents_ref, place_ref, owned_ref, plen_ref,
    q_ref, nk_ref, nv_ref, res_ref, gain_ref,
    hk_hbm, hv_hbm, pk_hbm, pv_hbm, wo_hbm, wq_hbm,
    qkv_out, res_out,
    qbuf, pbuf, obuf, hk, hv, pk, pv, wo, wq, base, acc,
    load_sem, qsend, qrecv, psend, precv, osend, orecv,
):
    rows, lanes = q_ref.shape
    heads = lanes // HEAD_DIM
    depth = res_ref.shape[1]
    chunk = depth // OUT_CHUNKS
    tokens = hk.shape[0]
    block_count = table_ref.shape[0]
    block = tokens // block_count
    outer, inner = grid_of(req_size)
    me = lax.axis_index("req")
    my_tp = lax.axis_index("tp")
    c = lax.rem(me, 2)
    i = lax.rem(me // 2, inner)
    o = me // (2 * inner)

    def at(oo, ii, cc):
        return (oo * inner + ii) * 2 + cc

    outer_peers = [at(lax.rem(o + d, outer), i, c) for d in range(1, outer)]
    inner_peers = [at(o, lax.rem(i + e, inner), c) for e in range(1, inner)]
    core_peer = at(o, i, 1 - c)
    tp_peers = [lax.rem(my_tp + d, tp_size) for d in range(1, tp_size)]

    barrier = pltpu.get_barrier_semaphore()
    for peer in outer_peers + inner_peers + [core_peer]:
        pl.semaphore_signal(barrier, inc=1, device_id={"req": peer}, device_id_type=pl.DeviceIdType.MESH)
    for peer in tp_peers:
        pl.semaphore_signal(barrier, inc=1, device_id={"tp": peer}, device_id_type=pl.DeviceIdType.MESH)

    loads = [
        pltpu.make_async_copy(src, dst, load_sem.at[n])
        for n, (src, dst) in enumerate(
            [(pk_hbm, pk), (pv_hbm, pv), (hk_hbm, hk), (hv_hbm, hv), (wo_hbm, wo), (wq_hbm, wq)]
        )
    ]
    for copy in loads:
        copy.start()
    qbuf[me] = q_ref[...]

    pl.semaphore_wait(barrier, len(outer_peers) + len(inner_peers) + 1 + len(tp_peers))

    def gather(buf, send, recv, between):
        sent = []

        def push(slot, peer):
            copy = pltpu.make_async_remote_copy(
                src_ref=buf.at[slot], dst_ref=buf.at[slot],
                send_sem=send.at[len(sent)], recv_sem=recv.at[slot],
                device_id={"req": peer}, device_id_type=pl.DeviceIdType.MESH,
            )
            copy.start()
            sent.append(copy)

        def arrive(slot):
            pltpu.make_async_remote_copy(
                src_ref=buf.at[slot], dst_ref=buf.at[slot],
                send_sem=send.at[0], recv_sem=recv.at[slot],
                device_id={"req": core_peer}, device_id_type=pl.DeviceIdType.MESH,
            ).wait_recv()

        for peer in reversed(outer_peers):
            push(me, peer)
        for peer in inner_peers + [core_peer]:
            push(me, peer)
        result = between()
        for d in range(1, outer):
            slot = at(lax.rem(o + d, outer), i, c)
            arrive(slot)
            for peer in inner_peers + [core_peer]:
                push(slot, peer)
        for e in range(1, inner):
            for d in range(outer):
                slot = at(lax.rem(o + d, outer), lax.rem(i + e, inner), c)
                arrive(slot)
                push(slot, core_peer)
        for e in range(inner):
            for d in range(outer):
                arrive(at(lax.rem(o + d, outer), lax.rem(i + e, inner), 1 - c))
        return result, sent

    def key_counts():
        lane = lax.broadcasted_iota(jnp.int32, (1, tokens), 1)
        lane_block = lane // block
        lane_pos = lane - lane_block * block
        for p in range(BEAMS):
            total = jnp.zeros((1, tokens), jnp.float32)
            for j in range(block_count):
                live = (lane_block == table_ref[j, p]) & (lane_pos + j * block < len_ref[p])
                total = total + jnp.where(live, 1.0, 0.0)
            base[p : p + 1, :] = total
        pool = base[...]
        row8 = lax.broadcasted_iota(jnp.int32, (BEAMS, BEAMS), 0)
        col8 = lax.broadcasted_iota(jnp.int32, (BEAMS, BEAMS), 1)
        new_row = lax.broadcasted_iota(jnp.int32, (BEAMS, rows), 0)
        new_col = lax.broadcasted_iota(jnp.int32, (BEAMS, rows), 1)
        new = jnp.zeros((BEAMS, rows), jnp.float32)
        pools, news = [], []
        for s in range(steps):
            pick = jnp.zeros((BEAMS, BEAMS), jnp.float32)
            for b in range(BEAMS):
                pick = jnp.where((row8 == b) & (col8 == parents_ref[s, b]), 1.0, pick)
            pool = jnp.dot(pick, pool, preferred_element_type=jnp.float32)
            new = jnp.dot(pick, new, preferred_element_type=jnp.float32)
            new = new + jnp.where(new_col == new_row + s * BEAMS, 1.0, 0.0)
            pools.append(pool)
            news.append(new)
        return jnp.concatenate(pools, axis=0), jnp.concatenate(news, axis=0)

    (pool_count, new_count), q_sent = gather(qbuf, qsend, qrecv, key_counts)

    loads[0].wait()
    loads[1].wait()
    asked = spread_heads(qbuf[owned_ref[0]], heads)
    scores = dot_t(asked, pk[...])
    prompt_lane = lax.broadcasted_iota(jnp.int32, scores.shape, 1)
    scores = jnp.where(prompt_lane < plen_ref[0], scores, NEG_FILL)
    top = jnp.max(scores, axis=1, keepdims=True)
    weights = jnp.exp(scores - top).astype(jnp.bfloat16)
    total = jnp.sum(weights.astype(jnp.float32), axis=1, keepdims=True)
    wide = jnp.dot(weights, pv[...], preferred_element_type=jnp.float32) / total
    log_total = top + jnp.log(total)
    stat_lane = lax.broadcasted_iota(jnp.int32, (rows, LANES), 1)
    stats = jnp.zeros((rows, LANES), jnp.float32)
    rest = log_total
    for part in range(3):
        level = rest.astype(jnp.bfloat16).astype(jnp.float32)
        rest = rest - level
        for h in range(heads):
            stats = jnp.where(stat_lane == part * heads + h, level[h * rows : (h + 1) * rows], stats)
    pbuf[me, :, :lanes] = own_columns(wide, rows, lanes).astype(jnp.bfloat16)
    pbuf[me, :, lanes:] = stats.astype(jnp.bfloat16)

    def home_part():
        loads[2].wait()
        loads[3].wait()
        query = spread_heads(q_ref[...], heads)
        pool_c = jnp.concatenate([pool_count] * heads, axis=0)
        new_c = jnp.concatenate([new_count] * heads, axis=0)
        pool_s = jnp.where(pool_c > 0.0, dot_t(query, hk[...]), NEG_FILL)
        new_s = jnp.where(new_c > 0.0, dot_t(query, nk_ref[...]), NEG_FILL)
        home_top = jnp.maximum(
            jnp.max(pool_s, axis=1, keepdims=True), jnp.max(new_s, axis=1, keepdims=True)
        )
        pool_w = jnp.exp(pool_s - home_top).astype(jnp.bfloat16).astype(jnp.float32) * pool_c
        new_w = jnp.exp(new_s - home_top).astype(jnp.bfloat16)
        home_sum = jnp.sum(pool_w, axis=1, keepdims=True) + jnp.sum(
            new_w.astype(jnp.float32), axis=1, keepdims=True
        )
        numer = jnp.dot(pool_w.astype(jnp.bfloat16), hv[...], preferred_element_type=jnp.float32)
        numer = numer + jnp.dot(new_w, nv_ref[...], preferred_element_type=jnp.float32)
        return home_top, home_sum, numer

    (home_top, home_sum, numer), p_sent = gather(pbuf, psend, precv, home_part)

    place = place_ref[0]
    reply = pbuf[place].astype(jnp.float32)
    stats = reply[:, lanes:]
    reply_log = []
    for h in range(heads):
        reply_log.append(
            stats[:, h : h + 1]
            + stats[:, heads + h : heads + h + 1]
            + stats[:, 2 * heads + h : 2 * heads + h + 1]
        )
    reply_log = jnp.concatenate(reply_log, axis=0)
    joint = jnp.maximum(home_top, reply_log)
    home_factor = jnp.exp(home_top - joint)
    prompt_factor = jnp.exp(reply_log - joint)
    scale = 1.0 / (home_sum * home_factor + prompt_factor)
    prompt_wide = jnp.concatenate([reply[:, :lanes]] * heads, axis=0)
    joined = numer * (home_factor * scale) + prompt_wide * (prompt_factor * scale)
    attended = own_columns(joined, rows, lanes).astype(jnp.bfloat16)

    loads[4].wait()
    o_sent = []
    for k in range(OUT_CHUNKS):
        cols = slice(k * chunk, (k + 1) * chunk)
        part = jnp.dot(attended, wo[:, cols], preferred_element_type=jnp.float32)
        obuf[my_tp, k] = part.astype(jnp.bfloat16)
        for peer in tp_peers:
            copy = pltpu.make_async_remote_copy(
                src_ref=obuf.at[my_tp, k], dst_ref=obuf.at[my_tp, k],
                send_sem=osend.at[len(o_sent)], recv_sem=orecv.at[my_tp, k],
                device_id={"tp": peer}, device_id_type=pl.DeviceIdType.MESH,
            )
            copy.start()
            o_sent.append(copy)

    loads[5].wait()
    square = jnp.zeros((rows, 1), jnp.float32)
    for k in range(OUT_CHUNKS):
        cols = slice(k * chunk, (k + 1) * chunk)
        for peer in tp_peers:
            pltpu.make_async_remote_copy(
                src_ref=obuf.at[peer, k], dst_ref=obuf.at[peer, k],
                send_sem=osend.at[0], recv_sem=orecv.at[peer, k],
                device_id={"tp": peer}, device_id_type=pl.DeviceIdType.MESH,
            ).wait_recv()
        summed = obuf[0, k].astype(jnp.float32)
        for t in range(1, tp_size):
            summed = summed + obuf[t, k].astype(jnp.float32)
        mixed = res_ref[:, cols].astype(jnp.float32) + summed
        res_out[:, cols] = mixed.astype(jnp.bfloat16)
        square = square + jnp.sum(mixed * mixed, axis=1, keepdims=True)
        gained = (mixed * gain_ref[:, cols].astype(jnp.float32)).astype(jnp.bfloat16)
        for n in range(3):
            term = jnp.dot(gained, wq[n, cols, :], preferred_element_type=jnp.float32)
            if k == 0:
                acc[n] = term
            else:
                acc[n] += term
    inverse = lax.rsqrt(square / depth + NORM_EPS)
    for n in range(3):
        scaled = acc[n] * inverse
        for s in range(steps):
            qkv_out[s, n] = scaled[s * BEAMS : (s + 1) * BEAMS].astype(jnp.bfloat16)

    for copy in q_sent + p_sent + o_sent:
        copy.wait_send()


def shards(
    queries, new_kv, residual, home_cache, prompt_cache, home_table, home_len,
    parents, prompt_place, owned_request, prompt_len, out_weight, norm_gain, qkv_weight,
):
    steps, beams, lanes = queries.shape
    rows = steps * beams
    depth = residual.shape[2]
    req_size = lax.axis_size("req")
    tp_size = lax.axis_size("tp")
    outer, inner = grid_of(req_size)
    tokens = home_cache.shape[0] * home_cache.shape[1]
    sends = (outer - 1) + outer * (inner - 1) + outer * inner
    smem = pl.BlockSpec(memory_space=pltpu.SMEM)
    vmem = pl.BlockSpec(memory_space=pltpu.VMEM)
    anym = pl.BlockSpec(memory_space=pl.ANY)
    wq = qkv_weight.transpose(1, 0, 2)
    bf16, f32 = jnp.bfloat16, jnp.float32
    dma = pltpu.SemaphoreType.DMA
    qkv, res = pl.pallas_call(
        functools.partial(kernel, req_size, tp_size, steps),
        out_shape=(
            jax.ShapeDtypeStruct((steps, 3, beams, lanes), bf16),
            jax.ShapeDtypeStruct((rows, depth), bf16),
        ),
        in_specs=[smem] * 6 + [vmem] * 5 + [anym] * 6,
        out_specs=(vmem, vmem),
        scratch_shapes=[
            pltpu.VMEM((req_size, rows, lanes), bf16),
            pltpu.VMEM((req_size, rows, lanes + LANES), bf16),
            pltpu.VMEM((tp_size, OUT_CHUNKS, rows, depth // OUT_CHUNKS), bf16),
            pltpu.VMEM((tokens, lanes), bf16),
            pltpu.VMEM((tokens, lanes), bf16),
            pltpu.VMEM((tokens, lanes), bf16),
            pltpu.VMEM((tokens, lanes), bf16),
            pltpu.VMEM(out_weight.shape, bf16),
            pltpu.VMEM(wq.shape, bf16),
            pltpu.VMEM((beams, tokens), f32),
            pltpu.VMEM((3, rows, lanes), f32),
            dma((6,)),
            dma((sends,)),
            dma((req_size,)),
            dma((sends,)),
            dma((req_size,)),
            dma((max(1, OUT_CHUNKS * (tp_size - 1)),)),
            dma((tp_size, OUT_CHUNKS)),
        ],
        compiler_params=pltpu.CompilerParams(
            collective_id=0, has_side_effects=True, vmem_limit_bytes=40 * 1024 * 1024
        ),
    )(
        home_table.T, home_len, parents, prompt_place, owned_request, prompt_len,
        queries.reshape(rows, lanes),
        new_kv[:, :, 0].reshape(rows, lanes),
        new_kv[:, :, 1].reshape(rows, lanes),
        residual.reshape(rows, depth),
        norm_gain.reshape(1, depth),
        home_cache[:, :, 0].reshape(tokens, lanes),
        home_cache[:, :, 1].reshape(tokens, lanes),
        prompt_cache[:, :, 0].reshape(tokens, lanes),
        prompt_cache[:, :, 1].reshape(tokens, lanes),
        out_weight,
        wq,
    )
    return qkv.transpose(0, 2, 1, 3), res.reshape(steps, beams, depth)


def solution(mesh):
    placed = (
        P(None, "req", "tp"),
        P(None, "req", None, "tp"),
        P(None, "req", None),
        P("req", None, None, "tp"),
        P("req", None, None, "tp"),
        P("req", None),
        P("req"),
        P(None, "req"),
        P("req"),
        P("req"),
        P("req"),
        P("tp", None),
        P(),
        P(None, None, "tp"),
    )
    return jax.shard_map(
        shards,
        mesh=mesh,
        in_specs=placed,
        out_specs=(P(None, "req", None, "tp"), P(None, "req", None)),
        check_vma=False,
    )
```

```python
import functools
import math

import jax
import jax.numpy as jnp
from jax import lax
from jax.experimental import pallas as pl
from jax.experimental.pallas import tpu as pltpu
from jax.sharding import PartitionSpec as P

HEAD_DIM = 64
BEAMS = 8
LANES = 128
OUT_CHUNKS = 4
SPLIT = 32

NEG_FILL = -1e30
NORM_EPS = 1e-05


def grid_of(req_size):
    chips = req_size // 2
    outer = 4 if chips % 4 == 0 else 1
    return outer, chips // outer


def spread_heads(q, heads):
    rows, lanes = q.shape
    scaled = q.astype(jnp.float32) * (1.0 / math.sqrt(HEAD_DIM))
    lane_head = lax.broadcasted_iota(jnp.int32, (rows, lanes), 1) // HEAD_DIM
    parts = [jnp.where(lane_head == h, scaled, 0.0) for h in range(heads)]
    return jnp.concatenate(parts, axis=0).astype(jnp.bfloat16)


def dot_t(a, b):
    return lax.dot_general(a, b, (((1,), (1,)), ((), ())), preferred_element_type=jnp.float32)


def own_columns(wide, rows, lanes):
    first = lax.broadcasted_iota(jnp.int32, (rows, LANES), 1) < HEAD_DIM
    tiles = []
    for t in range(lanes // LANES):
        cols = slice(t * LANES, (t + 1) * LANES)
        a = wide[2 * t * rows : (2 * t + 1) * rows, cols]
        b = wide[(2 * t + 1) * rows : (2 * t + 2) * rows, cols]
        tiles.append(jnp.where(first, a, b))
    return tiles[0] if len(tiles) == 1 else jnp.concatenate(tiles, axis=1)


def split_blocks(raw, keys, values):
    tokens, lanes = keys.shape
    kinds = 2 * (lanes // LANES)
    size = SPLIT * kinds
    out_row = lax.broadcasted_iota(jnp.int32, (size, size), 0)
    in_row = lax.broadcasted_iota(jnp.int32, (size, size), 1)
    wanted = (out_row % SPLIT) * kinds + out_row // SPLIT
    order = jnp.where(in_row == wanted, 1.0, 0.0).astype(jnp.bfloat16)
    for n in range(tokens // SPLIT):
        sorted_rows = jnp.dot(
            order, raw[n * size : (n + 1) * size, :], preferred_element_type=jnp.float32
        ).astype(jnp.bfloat16)
        for t in range(lanes // LANES):
            at = 2 * t * SPLIT
            rows, cols = slice(n * SPLIT, (n + 1) * SPLIT), slice(t * LANES, (t + 1) * LANES)
            keys[rows, cols] = sorted_rows[at : at + SPLIT]
            values[rows, cols] = sorted_rows[at + SPLIT : at + 2 * SPLIT]


def kernel(
    req_size, tp_size, steps,
    table_any, len_any, parents_any, place_any, owned_any, plen_any,
    q_any, new_any, res_any, gain_any, home_any, prompt_any, wo_any, wq_any,
    qkv_out, res_out,
    table_ref, len_ref, parents_ref, place_ref, owned_ref, plen_ref,
    q_ref, new_raw, res_ref, gain_ref, home_raw, prompt_raw, wo, wq,
    meta, qz, qmsg, qplane, rz, rmsg, rplane, obuf,
    nk, nv, hk, hv, pk, pv, base, acc,
    load_sem, msend, mrecv, qzsend, qzrecv, qpsend, qprecv,
    rzsend, rzrecv, rpsend, rprecv, osend, orecv,
):
    rows, lanes = q_ref.shape
    heads = lanes // HEAD_DIM
    depth = res_ref.shape[1]
    chunk = depth // OUT_CHUNKS
    tokens = hk.shape[0]
    block_count = table_ref.shape[0]
    block = tokens // block_count
    outer, inner = grid_of(req_size)
    planes = 2 * inner
    me = lax.axis_index("req")
    my_tp = lax.axis_index("tp")
    o = me // planes
    p = lax.rem(me, planes)

    mesh_id = pl.DeviceIdType.MESH
    outer_peers = [lax.rem(o + d, outer) * planes + p for d in range(1, outer)]
    plane_peers = [lax.rem(p + d, planes) for d in range(1, planes)]
    tp_peers = [lax.rem(my_tp + d, tp_size) for d in range(1, tp_size)]

    barrier = pltpu.get_barrier_semaphore()
    for peer in outer_peers + [o * planes + pp for pp in plane_peers]:
        pl.semaphore_signal(barrier, inc=1, device_id={"req": peer}, device_id_type=mesh_id)
    for peer in tp_peers:
        pl.semaphore_signal(barrier, inc=1, device_id={"tp": peer}, device_id_type=mesh_id)

    pairs = [
        (q_any, q_ref), (place_any, place_ref), (owned_any, owned_ref), (plen_any, plen_ref),
        (table_any, table_ref), (len_any, len_ref), (parents_any, parents_ref),
        (prompt_any, prompt_raw), (home_any, home_raw), (new_any, new_raw),
        (wo_any, wo), (res_any, res_ref), (gain_any, gain_ref), (wq_any, wq),
    ]
    loads = [pltpu.make_async_copy(src, dst, load_sem.at[n]) for n, (src, dst) in enumerate(pairs)]
    for copy in loads:
        copy.start()
    sent = []

    def push(src, dst, send_sem, recv_sem, axis, peer):
        copy = pltpu.make_async_remote_copy(
            src_ref=src, dst_ref=dst, send_sem=send_sem, recv_sem=recv_sem,
            device_id={axis: peer}, device_id_type=mesh_id,
        )
        copy.start()
        sent.append(copy)

    def arrive(dst, send_sem, recv_sem, axis, peer):
        pltpu.make_async_remote_copy(
            src_ref=dst, dst_ref=dst, send_sem=send_sem, recv_sem=recv_sem,
            device_id={axis: peer}, device_id_type=mesh_id,
        ).wait_recv()

    def send_outer(buf, send, recv):
        for d in reversed(range(1, outer)):
            push(buf.at[o], buf.at[o], send.at[d - 1], recv.at[o], "req", outer_peers[d - 1])

    def wait_outer(buf, send, recv):
        for d in range(1, outer):
            slot = lax.rem(o + d, outer)
            arrive(buf.at[slot], send.at[0], recv.at[slot], "req", outer_peers[d - 1])

    def send_plane(buf, marks, msg, landed, send, recv):
        held = [buf[s].astype(jnp.float32) for s in range(outer)]

        def chosen(target):
            value = held[0]
            for s in range(1, outer):
                value = jnp.where(marks[s] == target.astype(jnp.float32), held[s], value)
            return value.astype(jnp.bfloat16)

        for d, pp in enumerate(plane_peers):
            msg[d] = chosen(o * planes + pp)
            push(msg.at[d], landed.at[p], send.at[d], recv.at[p], "req", o * planes + pp)
        landed[p] = chosen(me)

    def wait_plane(landed, send, recv):
        for pp in plane_peers:
            arrive(landed.at[pp], send.at[0], recv.at[pp], "req", o * planes + pp)

    def key_counts():
        lane = lax.broadcasted_iota(jnp.int32, (1, tokens), 1)
        lane_block = lane // block
        lane_pos = lane - lane_block * block
        for b in range(BEAMS):
            total = jnp.zeros((1, tokens), jnp.float32)
            for j in range(block_count):
                live = (lane_block == table_ref[j, b]) & (lane_pos + j * block < len_ref[b])
                total = total + jnp.where(live, 1.0, 0.0)
            base[b : b + 1, :] = total
        pool = base[...]
        row8 = lax.broadcasted_iota(jnp.int32, (BEAMS, BEAMS), 0)
        col8 = lax.broadcasted_iota(jnp.int32, (BEAMS, BEAMS), 1)
        new_row = lax.broadcasted_iota(jnp.int32, (BEAMS, rows), 0)
        new_col = lax.broadcasted_iota(jnp.int32, (BEAMS, rows), 1)
        new = jnp.zeros((BEAMS, rows), jnp.float32)
        pools, news = [], []
        for s in range(steps):
            pick = jnp.zeros((BEAMS, BEAMS), jnp.float32)
            for b in range(BEAMS):
                pick = jnp.where((row8 == b) & (col8 == parents_ref[s, b]), 1.0, pick)
            pool = jnp.dot(pick, pool, preferred_element_type=jnp.float32)
            new = jnp.dot(pick, new, preferred_element_type=jnp.float32)
            new = new + jnp.where(new_col == new_row + s * BEAMS, 1.0, 0.0)
            pools.append(pool)
            news.append(new)
        return jnp.concatenate(pools, axis=0), jnp.concatenate(news, axis=0)

    for copy in loads[:7]:
        copy.wait()
    meta_lane = lax.broadcasted_iota(jnp.int32, (16, LANES), 1)
    meta[o] = (
        jnp.where(meta_lane < LANES // 2, place_ref[0], owned_ref[0])
        .astype(jnp.float32)
        .astype(jnp.bfloat16)
    )
    qz[o] = q_ref[...]
    pl.semaphore_wait(barrier, len(outer_peers) + len(plane_peers) + len(tp_peers))
    send_outer(meta, msend, mrecv)
    send_outer(qz, qzsend, qzrecv)
    pool_count, new_count = key_counts()
    loads[7].wait()
    split_blocks(prompt_raw, pk, pv)
    wait_outer(meta, msend, mrecv)
    marks = [meta[s].astype(jnp.float32) for s in range(outer)]
    place_marks = [mark[0:1, 0:1] for mark in marks]
    owned_marks = [mark[0:1, LANES // 2 : LANES // 2 + 1] for mark in marks]
    wait_outer(qz, qzsend, qzrecv)
    send_plane(qz, place_marks, qmsg, qplane, qpsend, qprecv)
    loads[8].wait()
    loads[9].wait()
    split_blocks(home_raw, hk, hv)
    split_blocks(new_raw, nk, nv)
    wait_plane(qplane, qpsend, qprecv)

    asked = spread_heads(qplane[lax.rem(owned_ref[0], planes)], heads)
    scores = dot_t(asked, pk[...])
    prompt_lane = lax.broadcasted_iota(jnp.int32, scores.shape, 1)
    scores = jnp.where(prompt_lane < plen_ref[0], scores, NEG_FILL)
    top = jnp.max(scores, axis=1, keepdims=True)
    weights = jnp.exp(scores - top).astype(jnp.bfloat16)
    total = jnp.sum(weights.astype(jnp.float32), axis=1, keepdims=True)
    wide = jnp.dot(weights, pv[...], preferred_element_type=jnp.float32) / total
    log_total = top + jnp.log(total)
    stat_lane = lax.broadcasted_iota(jnp.int32, (rows, LANES), 1)
    stats = jnp.zeros((rows, LANES), jnp.float32)
    rest = log_total
    for part in range(3):
        level = rest.astype(jnp.bfloat16).astype(jnp.float32)
        rest = rest - level
        for h in range(heads):
            stats = jnp.where(stat_lane == part * heads + h, level[h * rows : (h + 1) * rows], stats)
    rz[o, :, :lanes] = own_columns(wide, rows, lanes).astype(jnp.bfloat16)
    rz[o, :, lanes:] = stats.astype(jnp.bfloat16)
    send_outer(rz, rzsend, rzrecv)

    query = spread_heads(q_ref[...], heads)
    pool_c = jnp.concatenate([pool_count] * heads, axis=0)
    new_c = jnp.concatenate([new_count] * heads, axis=0)
    pool_s = jnp.where(pool_c > 0.0, dot_t(query, hk[...]), NEG_FILL)
    new_s = jnp.where(new_c > 0.0, dot_t(query, nk[...]), NEG_FILL)
    home_top = jnp.maximum(
        jnp.max(pool_s, axis=1, keepdims=True), jnp.max(new_s, axis=1, keepdims=True)
    )
    pool_w = jnp.exp(pool_s - home_top).astype(jnp.bfloat16).astype(jnp.float32) * pool_c
    new_w = jnp.exp(new_s - home_top).astype(jnp.bfloat16)
    home_sum = jnp.sum(pool_w, axis=1, keepdims=True) + jnp.sum(
        new_w.astype(jnp.float32), axis=1, keepdims=True
    )
    numer = jnp.dot(pool_w.astype(jnp.bfloat16), hv[...], preferred_element_type=jnp.float32)
    numer = numer + jnp.dot(new_w, nv[...], preferred_element_type=jnp.float32)

    wait_outer(rz, rzsend, rzrecv)
    send_plane(rz, owned_marks, rmsg, rplane, rpsend, rprecv)
    wait_plane(rplane, rpsend, rprecv)
    reply = rplane[lax.rem(place_ref[0], planes)].astype(jnp.float32)
    stats = reply[:, lanes:]
    reply_log = []
    for h in range(heads):
        reply_log.append(
            stats[:, h : h + 1]
            + stats[:, heads + h : heads + h + 1]
            + stats[:, 2 * heads + h : 2 * heads + h + 1]
        )
    reply_log = jnp.concatenate(reply_log, axis=0)
    joint = jnp.maximum(home_top, reply_log)
    home_factor = jnp.exp(home_top - joint)
    prompt_factor = jnp.exp(reply_log - joint)
    scale = 1.0 / (home_sum * home_factor + prompt_factor)
    prompt_wide = jnp.concatenate([reply[:, :lanes]] * heads, axis=0)
    joined = numer * (home_factor * scale) + prompt_wide * (prompt_factor * scale)
    attended = own_columns(joined, rows, lanes).astype(jnp.bfloat16)

    loads[10].wait()
    for k in range(OUT_CHUNKS):
        cols = slice(k * chunk, (k + 1) * chunk)
        part = jnp.dot(attended, wo[:, cols], preferred_element_type=jnp.float32)
        obuf[my_tp, k] = part.astype(jnp.bfloat16)
        for d, peer in enumerate(tp_peers):
            mine = obuf.at[my_tp, k]
            push(mine, mine, osend.at[k * len(tp_peers) + d], orecv.at[my_tp, k], "tp", peer)

    for copy in loads[11:]:
        copy.wait()
    square = jnp.zeros((rows, 1), jnp.float32)
    for k in range(OUT_CHUNKS):
        cols = slice(k * chunk, (k + 1) * chunk)
        for peer in tp_peers:
            arrive(obuf.at[peer, k], osend.at[0], orecv.at[peer, k], "tp", peer)
        summed = obuf[0, k].astype(jnp.float32)
        for t in range(1, tp_size):
            summed = summed + obuf[t, k].astype(jnp.float32)
        mixed = res_ref[:, cols].astype(jnp.float32) + summed
        res_out[:, cols] = mixed.astype(jnp.bfloat16)
        square = square + jnp.sum(mixed * mixed, axis=1, keepdims=True)
        gained = (mixed * gain_ref[:, cols].astype(jnp.float32)).astype(jnp.bfloat16)
        for n in range(3):
            term = jnp.dot(gained, wq[n, cols, :], preferred_element_type=jnp.float32)
            if k == 0:
                acc[n] = term
            else:
                acc[n] += term
    inverse = lax.rsqrt(square / depth + NORM_EPS)
    for n in range(3):
        scaled = acc[n] * inverse
        for s in range(steps):
            qkv_out[s, n] = scaled[s * BEAMS : (s + 1) * BEAMS].astype(jnp.bfloat16)

    for copy in sent:
        copy.wait_send()


def token_rows(cache):
    lanes = cache.shape[-1]
    tiles = cache.reshape(-1, 2, lanes // LANES, LANES).transpose(0, 2, 1, 3)
    return tiles.reshape(-1, LANES)


def shards(
    queries, new_kv, residual, home_cache, prompt_cache, home_table, home_len,
    parents, prompt_place, owned_request, prompt_len, out_weight, norm_gain, qkv_weight,
):
    steps, beams, lanes = queries.shape
    rows = steps * beams
    depth = residual.shape[2]
    req_size = lax.axis_size("req")
    tp_size = lax.axis_size("tp")
    outer, inner = grid_of(req_size)
    planes = 2 * inner
    tokens = home_cache.shape[0] * home_cache.shape[1]
    vmem = pl.BlockSpec(memory_space=pltpu.VMEM)
    hbm = pl.BlockSpec(memory_space=pltpu.HBM)
    bf16, f32 = jnp.bfloat16, jnp.float32
    dma = pltpu.SemaphoreType.DMA
    ints = (home_table.T, home_len, parents, prompt_place, owned_request, prompt_len)
    floats = (
        queries.reshape(rows, lanes),
        token_rows(new_kv),
        residual.reshape(rows, depth),
        norm_gain.reshape(1, depth),
        token_rows(home_cache),
        token_rows(prompt_cache),
        out_weight,
        qkv_weight.transpose(1, 0, 2),
    )
    wide = lanes + LANES
    sems = [
        (len(ints) + len(floats),),
        (outer,), (outer,), (outer,), (outer,), (planes,), (planes,),
        (outer,), (outer,), (planes,), (planes,),
        (OUT_CHUNKS * tp_size,), (tp_size, OUT_CHUNKS),
    ]
    qkv, res = pl.pallas_call(
        functools.partial(kernel, req_size, tp_size, steps),
        out_shape=(
            jax.ShapeDtypeStruct((steps, 3, beams, lanes), bf16),
            jax.ShapeDtypeStruct((rows, depth), bf16),
        ),
        in_specs=[hbm] * (len(ints) + len(floats)),
        out_specs=(vmem, vmem),
        scratch_shapes=[pltpu.SMEM(a.shape, jnp.int32) for a in ints]
        + [pltpu.VMEM(a.shape, bf16) for a in floats]
        + [
            pltpu.VMEM((outer, 16, LANES), bf16),
            pltpu.VMEM((outer, rows, lanes), bf16),
            pltpu.VMEM((planes - 1, rows, lanes), bf16),
            pltpu.VMEM((planes, rows, lanes), bf16),
            pltpu.VMEM((outer, rows, wide), bf16),
            pltpu.VMEM((planes - 1, rows, wide), bf16),
            pltpu.VMEM((planes, rows, wide), bf16),
            pltpu.VMEM((tp_size, OUT_CHUNKS, rows, depth // OUT_CHUNKS), bf16),
            pltpu.VMEM((rows, lanes), bf16),
            pltpu.VMEM((rows, lanes), bf16),
            pltpu.VMEM((tokens, lanes), bf16),
            pltpu.VMEM((tokens, lanes), bf16),
            pltpu.VMEM((tokens, lanes), bf16),
            pltpu.VMEM((tokens, lanes), bf16),
            pltpu.VMEM((beams, tokens), f32),
            pltpu.VMEM((3, rows, lanes), f32),
        ]
        + [dma(shape) for shape in sems],
        compiler_params=pltpu.CompilerParams(
            collective_id=0, has_side_effects=True, vmem_limit_bytes=56 * 1024 * 1024
        ),
    )(*ints, *floats)
    return qkv.transpose(0, 2, 1, 3), res.reshape(steps, beams, depth)


def solution(mesh):
    placed = (
        P(None, "req", "tp"),
        P(None, "req", None, "tp"),
        P(None, "req", None),
        P("req", None, None, "tp"),
        P("req", None, None, "tp"),
        P("req", None),
        P("req"),
        P(None, "req"),
        P("req"),
        P("req"),
        P("req"),
        P("tp", None),
        P(),
        P(None, None, "tp"),
    )
    return jax.shard_map(
        shards,
        mesh=mesh,
        in_specs=placed,
        out_specs=(P(None, "req", None, "tp"), P(None, "req", None)),
        check_vma=False,
    )
```

```python
import functools
import math

import jax
import jax.numpy as jnp
from jax import lax
from jax.experimental import pallas as pl
from jax.experimental.pallas import tpu as pltpu
from jax.sharding import PartitionSpec as P

HEAD_DIM = 64
BEAMS = 8
LANES = 128
OUT_CHUNKS = 4
SPLIT = 32

NEG_FILL = -1e30
NORM_EPS = 1e-05


def grid_of(req_size):
    chips = req_size // 2
    outer = 4 if chips % 4 == 0 else 1
    return outer, chips // outer


def spread_heads(q, heads):
    rows, lanes = q.shape
    scaled = q.astype(jnp.float32) * (1.0 / math.sqrt(HEAD_DIM))
    lane_head = lax.broadcasted_iota(jnp.int32, (rows, lanes), 1) // HEAD_DIM
    parts = [jnp.where(lane_head == h, scaled, 0.0) for h in range(heads)]
    return jnp.concatenate(parts, axis=0).astype(jnp.bfloat16)


def dot_t(a, b):
    return lax.dot_general(a, b, (((1,), (1,)), ((), ())), preferred_element_type=jnp.float32)


def own_columns(rows, lanes, piece):
    first = lax.broadcasted_iota(jnp.int32, (rows, LANES), 1) < HEAD_DIM
    tiles = []
    for t in range(lanes // LANES):
        cols = slice(t * LANES, (t + 1) * LANES)
        tiles.append(jnp.where(first, piece(2 * t, cols), piece(2 * t + 1, cols)))
    return tiles[0] if len(tiles) == 1 else jnp.concatenate(tiles, axis=1)


def split_blocks(raw, keys, values):
    tokens, lanes = keys.shape
    kinds = 2 * (lanes // LANES)
    size = SPLIT * kinds
    out_row = lax.broadcasted_iota(jnp.int32, (size, size), 0)
    in_row = lax.broadcasted_iota(jnp.int32, (size, size), 1)
    wanted = (out_row % SPLIT) * kinds + out_row // SPLIT
    order = jnp.where(in_row == wanted, 1.0, 0.0).astype(jnp.bfloat16)
    for n in range(tokens // SPLIT):
        sorted_rows = jnp.dot(
            order, raw[n * size : (n + 1) * size, :], preferred_element_type=jnp.float32
        ).astype(jnp.bfloat16)
        for t in range(lanes // LANES):
            at = 2 * t * SPLIT
            rows, cols = slice(n * SPLIT, (n + 1) * SPLIT), slice(t * LANES, (t + 1) * LANES)
            keys[rows, cols] = sorted_rows[at : at + SPLIT]
            values[rows, cols] = sorted_rows[at + SPLIT : at + 2 * SPLIT]


def kernel(
    req_size, tp_size, steps,
    place_ref, owned_ref, plen_ref, table_any, len_any, parents_any,
    q_any, new_any, res_any, gain_any, home_any, prompt_any, wo_any, wq_any,
    qkv_out, res_out,
    table_ref, len_ref, parents_ref,
    q_ref, new_raw, res_ref, gain_ref, home_raw, prompt_raw, wo, wq,
    meta_c, meta_p, qa, qa_msg, qa_in, qb, qb_msg, qb_in, ra, ra_msg, ra_in, rb, rb_msg, rb_in, obuf,
    nk, nv, hk, hv, pk, pv, base, acc,
    load_sem, osend, orecv, *hop_sems
):
    rows, lanes = q_ref.shape
    heads = lanes // HEAD_DIM
    depth = res_ref.shape[1]
    chunk = depth // OUT_CHUNKS
    tokens = hk.shape[0]
    block_count = table_ref.shape[0]
    block = tokens // block_count
    outer, inner = grid_of(req_size)
    planes = 2 * inner
    me = lax.axis_index("req")
    my_tp = lax.axis_index("tp")
    o = me // planes
    p = lax.rem(me, planes)

    half = rows // 2
    mesh_id = pl.DeviceIdType.MESH
    column = (outer, o, lambda n: n * planes + p)
    plane = (planes, p, lambda n: o * planes + n)

    def others(group):
        size, mine, _ = group
        return [lax.rem(mine + d, size) for d in range(1, size)]

    sem_pairs = [hop_sems[n : n + 2] for n in range(0, len(hop_sems), 2)]
    meta_c_sem, meta_p_sem, qa_sem, qa2_sem, qb_sem, qb2_sem, ra_sem, ra2_sem, rb_sem, rb2_sem = sem_pairs
    tp_peers = [lax.rem(my_tp + d, tp_size) for d in range(1, tp_size)]

    barrier = pltpu.get_barrier_semaphore()
    for group in (column, plane):
        for n in others(group):
            pl.semaphore_signal(barrier, inc=1, device_id={"req": group[2](n)}, device_id_type=mesh_id)
    for peer in tp_peers:
        pl.semaphore_signal(barrier, inc=1, device_id={"tp": peer}, device_id_type=mesh_id)

    pairs = [
        (q_any, q_ref), (table_any, table_ref), (len_any, len_ref), (parents_any, parents_ref),
        (prompt_any, prompt_raw), (home_any, home_raw), (new_any, new_raw),
        (wo_any, wo), (res_any, res_ref), (gain_any, gain_ref), (wq_any, wq),
    ]
    loads = [pltpu.make_async_copy(src, dst, load_sem.at[n]) for n, (src, dst) in enumerate(pairs)]
    for copy in loads:
        copy.start()
    sent = []

    def push(src, dst, send_sem, recv_sem, axis, peer):
        copy = pltpu.make_async_remote_copy(
            src_ref=src, dst_ref=dst, send_sem=send_sem, recv_sem=recv_sem,
            device_id={axis: peer}, device_id_type=mesh_id,
        )
        copy.start()
        sent.append(copy)

    def arrive(dst, send_sem, recv_sem, axis, peer):
        pltpu.make_async_remote_copy(
            src_ref=dst, dst_ref=dst, send_sem=send_sem, recv_sem=recv_sem,
            device_id={axis: peer}, device_id_type=mesh_id,
        ).wait_recv()

    def first_hop(buf, group, sems):
        _, mine, index = group
        for d, n in enumerate(others(group)):
            push(buf.at[mine], buf.at[mine], sems[0].at[d], sems[1].at[mine], "req", index(n))

    def wait_hop(buf, group, sems):
        for n in others(group):
            arrive(buf.at[n], sems[0].at[0], sems[1].at[n], "req", group[2](n))

    def second_hop(buf, marks, msg, landed, group, sems):
        held = [buf[s].astype(jnp.float32) for s in range(buf.shape[0])]
        _, mine, index = group

        def chosen(target):
            value = held[0]
            for s in range(1, len(held)):
                value = jnp.where(marks[s] == target.astype(jnp.float32), held[s], value)
            return value.astype(jnp.bfloat16)

        for d, n in enumerate(others(group)):
            msg[d] = chosen(index(n))
            push(msg.at[d], landed.at[mine], sems[0].at[d], sems[1].at[mine], "req", index(n))
        landed[mine] = chosen(me)

    def key_counts():
        lane = lax.broadcasted_iota(jnp.int32, (1, tokens), 1)
        lane_block = lane // block
        lane_pos = lane - lane_block * block
        for b in range(BEAMS):
            total = jnp.zeros((1, tokens), jnp.float32)
            for j in range(block_count):
                live = (lane_block == table_ref[j, b]) & (lane_pos + j * block < len_ref[b])
                total = total + jnp.where(live, 1.0, 0.0)
            base[b : b + 1, :] = total
        pool = base[...]
        row8 = lax.broadcasted_iota(jnp.int32, (BEAMS, BEAMS), 0)
        col8 = lax.broadcasted_iota(jnp.int32, (BEAMS, BEAMS), 1)
        new_row = lax.broadcasted_iota(jnp.int32, (BEAMS, rows), 0)
        new_col = lax.broadcasted_iota(jnp.int32, (BEAMS, rows), 1)
        new = jnp.zeros((BEAMS, rows), jnp.float32)
        pools, news = [], []
        for s in range(steps):
            pick = jnp.zeros((BEAMS, BEAMS), jnp.float32)
            for b in range(BEAMS):
                pick = jnp.where((row8 == b) & (col8 == parents_ref[s, b]), 1.0, pick)
            pool = jnp.dot(pick, pool, preferred_element_type=jnp.float32)
            new = jnp.dot(pick, new, preferred_element_type=jnp.float32)
            new = new + jnp.where(new_col == new_row + s * BEAMS, 1.0, 0.0)
            pools.append(pool)
            news.append(new)
        return jnp.concatenate(pools, axis=0), jnp.concatenate(news, axis=0)

    for copy in loads[:4]:
        copy.wait()
    meta_lane = lax.broadcasted_iota(jnp.int32, (16, LANES), 1)
    mark = (
        jnp.where(meta_lane < LANES // 2, place_ref[0], owned_ref[0])
        .astype(jnp.float32)
        .astype(jnp.bfloat16)
    )
    meta_c[o] = mark
    meta_p[p] = mark
    qa[o] = q_ref[:half, :]
    qb[p] = q_ref[half:, :]
    pl.semaphore_wait(barrier, outer - 1 + planes - 1 + len(tp_peers))
    first_hop(meta_p, plane, meta_p_sem)
    first_hop(qb, plane, qb_sem)
    first_hop(meta_c, column, meta_c_sem)
    first_hop(qa, column, qa_sem)
    pool_count, new_count = key_counts()

    def marks_of(meta):
        rows_of = [meta[s].astype(jnp.float32) for s in range(meta.shape[0])]
        middle = LANES // 2
        return [r[0:1, 0:1] for r in rows_of], [r[0:1, middle : middle + 1] for r in rows_of]

    wait_hop(meta_p, plane, meta_p_sem)
    places_p, owners_p = marks_of(meta_p)
    wait_hop(qb, plane, qb_sem)
    second_hop(qb, places_p, qb_msg, qb_in, column, qb2_sem)
    loads[4].wait()
    split_blocks(prompt_raw, pk, pv)
    wait_hop(meta_c, column, meta_c_sem)
    places_c, owners_c = marks_of(meta_c)
    wait_hop(qa, column, qa_sem)
    second_hop(qa, places_c, qa_msg, qa_in, plane, qa2_sem)
    loads[5].wait()
    loads[6].wait()
    split_blocks(home_raw, hk, hv)
    split_blocks(new_raw, nk, nv)
    wait_hop(qa_in, plane, qa2_sem)
    wait_hop(qb_in, column, qb2_sem)

    owned = owned_ref[0]
    asked = jnp.concatenate([qa_in[lax.rem(owned, planes)], qb_in[owned // planes]], axis=0)
    asked = spread_heads(asked, heads)
    scores = dot_t(asked, pk[...])
    prompt_lane = lax.broadcasted_iota(jnp.int32, scores.shape, 1)
    scores = jnp.where(prompt_lane < plen_ref[0], scores, NEG_FILL)
    top = jnp.max(scores, axis=1, keepdims=True)
    weights = jnp.exp(scores - top).astype(jnp.bfloat16)
    total = jnp.sum(weights.astype(jnp.float32), axis=1, keepdims=True)
    wide = jnp.dot(weights, pv[...], preferred_element_type=jnp.float32)
    part_of = 1.0 / total
    log_total = top + jnp.log(total)
    stat_lane = lax.broadcasted_iota(jnp.int32, (rows, LANES), 1)
    stats = jnp.zeros((rows, LANES), jnp.float32)
    rest = log_total
    for part in range(3):
        level = rest.astype(jnp.bfloat16).astype(jnp.float32)
        rest = rest - level
        for h in range(heads):
            stats = jnp.where(stat_lane == part * heads + h, level[h * rows : (h + 1) * rows], stats)
    def answer(h, cols):
        own = slice(h * rows, (h + 1) * rows)
        return wide[own, cols] * part_of[own]

    answers = own_columns(rows, lanes, answer).astype(jnp.bfloat16)
    stats = stats.astype(jnp.bfloat16)
    rb[p, :, :lanes] = answers[half:]
    rb[p, :, lanes:] = stats[half:]
    ra[o, :, :lanes] = answers[:half]
    ra[o, :, lanes:] = stats[:half]
    first_hop(rb, plane, rb_sem)
    first_hop(ra, column, ra_sem)

    wait_hop(rb, plane, rb_sem)
    second_hop(rb, owners_p, rb_msg, rb_in, column, rb2_sem)
    query = spread_heads(q_ref[...], heads)
    pool_c = jnp.concatenate([pool_count] * heads, axis=0)
    new_c = jnp.concatenate([new_count] * heads, axis=0)
    pool_s = jnp.where(pool_c > 0.0, dot_t(query, hk[...]), NEG_FILL)
    new_s = jnp.where(new_c > 0.0, dot_t(query, nk[...]), NEG_FILL)
    home_top = jnp.maximum(
        jnp.max(pool_s, axis=1, keepdims=True), jnp.max(new_s, axis=1, keepdims=True)
    )
    pool_w = jnp.exp(pool_s - home_top).astype(jnp.bfloat16).astype(jnp.float32) * pool_c
    new_w = jnp.exp(new_s - home_top).astype(jnp.bfloat16)
    home_sum = jnp.sum(pool_w, axis=1, keepdims=True) + jnp.sum(
        new_w.astype(jnp.float32), axis=1, keepdims=True
    )
    numer = jnp.dot(pool_w.astype(jnp.bfloat16), hv[...], preferred_element_type=jnp.float32)
    numer = numer + jnp.dot(new_w, nv[...], preferred_element_type=jnp.float32)

    wait_hop(ra, column, ra_sem)
    second_hop(ra, owners_c, ra_msg, ra_in, plane, ra2_sem)
    wait_hop(ra_in, plane, ra2_sem)
    wait_hop(rb_in, column, rb2_sem)
    place = place_ref[0]
    reply = jnp.concatenate([ra_in[lax.rem(place, planes)], rb_in[place // planes]], axis=0)
    reply = reply.astype(jnp.float32)
    stats = reply[:, lanes:]
    reply_log = []
    for h in range(heads):
        reply_log.append(
            stats[:, h : h + 1]
            + stats[:, heads + h : heads + h + 1]
            + stats[:, 2 * heads + h : 2 * heads + h + 1]
        )
    reply_log = jnp.concatenate(reply_log, axis=0)
    joint = jnp.maximum(home_top, reply_log)
    home_factor = jnp.exp(home_top - joint)
    prompt_factor = jnp.exp(reply_log - joint)
    scale = 1.0 / (home_sum * home_factor + prompt_factor)
    home_factor = home_factor * scale
    prompt_factor = prompt_factor * scale

    def joined(h, cols):
        own = slice(h * rows, (h + 1) * rows)
        return numer[own, cols] * home_factor[own] + reply[:, cols] * prompt_factor[own]

    attended = own_columns(rows, lanes, joined).astype(jnp.bfloat16)

    loads[7].wait()
    for k in range(OUT_CHUNKS):
        cols = slice(k * chunk, (k + 1) * chunk)
        part = jnp.dot(attended, wo[:, cols], preferred_element_type=jnp.float32)
        obuf[my_tp, k] = part.astype(jnp.bfloat16)
        for d, peer in enumerate(tp_peers):
            mine = obuf.at[my_tp, k]
            push(mine, mine, osend.at[k * len(tp_peers) + d], orecv.at[my_tp, k], "tp", peer)

    for copy in loads[8:]:
        copy.wait()
    gain_all = gain_ref[...].astype(jnp.float32)
    square = jnp.zeros((rows, 1), jnp.float32)
    for k in range(OUT_CHUNKS):
        cols = slice(k * chunk, (k + 1) * chunk)
        for peer in tp_peers:
            arrive(obuf.at[peer, k], osend.at[0], orecv.at[peer, k], "tp", peer)
        summed = obuf[0, k].astype(jnp.float32)
        for t in range(1, tp_size):
            summed = summed + obuf[t, k].astype(jnp.float32)
        mixed = res_ref[:, cols].astype(jnp.float32) + summed
        res_out[:, cols] = mixed.astype(jnp.bfloat16)
        square = square + jnp.sum(mixed * mixed, axis=1, keepdims=True)
        gain_rows = [gain_all[n : n + 1] for n in range(k * chunk // LANES, (k + 1) * chunk // LANES)]
        gained = (mixed * jnp.concatenate(gain_rows, axis=1)).astype(jnp.bfloat16)
        for n in range(3):
            term = jnp.dot(gained, wq[n, cols, :], preferred_element_type=jnp.float32)
            if k == 0:
                acc[n] = term
            else:
                acc[n] += term
    inverse = lax.rsqrt(square / depth + NORM_EPS)
    for n in range(3):
        scaled = acc[n] * inverse
        for s in range(steps):
            qkv_out[s, n] = scaled[s * BEAMS : (s + 1) * BEAMS].astype(jnp.bfloat16)

    for copy in sent:
        copy.wait_send()


def token_rows(cache):
    lanes = cache.shape[-1]
    tiles = cache.reshape(-1, 2, lanes // LANES, LANES).transpose(0, 2, 1, 3)
    return tiles.reshape(-1, LANES)


def shards(
    queries, new_kv, residual, home_cache, prompt_cache, home_table, home_len,
    parents, prompt_place, owned_request, prompt_len, out_weight, norm_gain, qkv_weight,
):
    steps, beams, lanes = queries.shape
    rows = steps * beams
    depth = residual.shape[2]
    req_size = lax.axis_size("req")
    tp_size = lax.axis_size("tp")
    outer, inner = grid_of(req_size)
    planes = 2 * inner
    tokens = home_cache.shape[0] * home_cache.shape[1]
    smem = pl.BlockSpec(memory_space=pltpu.SMEM)
    vmem = pl.BlockSpec(memory_space=pltpu.VMEM)
    hbm = pl.BlockSpec(memory_space=pltpu.HBM)
    bf16, f32 = jnp.bfloat16, jnp.float32
    dma = pltpu.SemaphoreType.DMA
    singles = (prompt_place, owned_request, prompt_len)
    ints = (home_table.T, home_len, parents)
    floats = (
        queries.reshape(rows, lanes),
        token_rows(new_kv),
        residual.reshape(rows, depth),
        norm_gain.reshape(-1, LANES),
        token_rows(home_cache),
        token_rows(prompt_cache),
        out_weight,
        qkv_weight.transpose(1, 0, 2),
    )
    wide = lanes + LANES
    half = rows // 2

    def route(first, second, width):
        return [
            pltpu.VMEM((first, half, width), bf16),
            pltpu.VMEM((second - 1, half, width), bf16),
            pltpu.VMEM((second, half, width), bf16),
        ]

    hops = [outer, planes] + [outer, planes, planes, outer] * 2
    sems = [(len(ints) + len(floats),), (OUT_CHUNKS * tp_size,), (tp_size, OUT_CHUNKS)]
    sems += [(size,) for size in hops for _ in range(2)]
    qkv, res = pl.pallas_call(
        functools.partial(kernel, req_size, tp_size, steps),
        out_shape=(
            jax.ShapeDtypeStruct((steps, 3, beams, lanes), bf16),
            jax.ShapeDtypeStruct((rows, depth), bf16),
        ),
        in_specs=[smem] * len(singles) + [hbm] * (len(ints) + len(floats)),
        out_specs=(vmem, vmem),
        scratch_shapes=[pltpu.SMEM(a.shape, jnp.int32) for a in ints]
        + [pltpu.VMEM(a.shape, bf16) for a in floats]
        + [
            pltpu.VMEM((outer, 16, LANES), bf16),
            pltpu.VMEM((planes, 16, LANES), bf16),
        ]
        + route(outer, planes, lanes)
        + route(planes, outer, lanes)
        + route(outer, planes, wide)
        + route(planes, outer, wide)
        + [
            pltpu.VMEM((tp_size, OUT_CHUNKS, rows, depth // OUT_CHUNKS), bf16),
            pltpu.VMEM((rows, lanes), bf16),
            pltpu.VMEM((rows, lanes), bf16),
            pltpu.VMEM((tokens, lanes), bf16),
            pltpu.VMEM((tokens, lanes), bf16),
            pltpu.VMEM((tokens, lanes), bf16),
            pltpu.VMEM((tokens, lanes), bf16),
            pltpu.VMEM((beams, tokens), f32),
            pltpu.VMEM((3, rows, lanes), f32),
        ]
        + [dma(shape) for shape in sems],
        compiler_params=pltpu.CompilerParams(
            collective_id=0, has_side_effects=True, vmem_limit_bytes=40 * 1024 * 1024
        ),
    )(*singles, *(pltpu.with_memory_space_constraint(x, pltpu.HBM) for x in ints + floats))
    return qkv.transpose(0, 2, 1, 3), res.reshape(steps, beams, depth)


def solution(mesh):
    placed = (
        P(None, "req", "tp"),
        P(None, "req", None, "tp"),
        P(None, "req", None),
        P("req", None, None, "tp"),
        P("req", None, None, "tp"),
        P("req", None),
        P("req"),
        P(None, "req"),
        P("req"),
        P("req"),
        P("req"),
        P("tp", None),
        P(),
        P(None, None, "tp"),
    )
    return jax.shard_map(
        shards,
        mesh=mesh,
        in_specs=placed,
        out_specs=(P(None, "req", None, "tp"), P(None, "req", None)),
        check_vma=False,
    )
```

```python
import functools
import math

import jax
import jax.numpy as jnp
from jax import lax
from jax.experimental import pallas as pl
from jax.experimental.pallas import tpu as pltpu
from jax.sharding import PartitionSpec as P

HEAD_DIM = 64
BEAMS = 8
LANES = 128
OUT_CHUNKS = 4
SPLIT = 32

NEG_FILL = -1e30
NORM_EPS = 1e-05


def grid_of(req_size):
    chips = req_size // 2
    outer = 4 if chips % 4 == 0 else 1
    return outer, chips // outer


def spread_heads(q, heads):
    rows, lanes = q.shape
    scaled = q.astype(jnp.float32) * (1.0 / math.sqrt(HEAD_DIM))
    lane_head = lax.broadcasted_iota(jnp.int32, (rows, lanes), 1) // HEAD_DIM
    parts = [jnp.where(lane_head == h, scaled, 0.0) for h in range(heads)]
    return jnp.concatenate(parts, axis=0).astype(jnp.bfloat16)


def dot_t(a, b):
    return lax.dot_general(a, b, (((1,), (1,)), ((), ())), preferred_element_type=jnp.float32)


def own_columns(rows, lanes, piece):
    first = lax.broadcasted_iota(jnp.int32, (rows, LANES), 1) < HEAD_DIM
    tiles = []
    for t in range(lanes // LANES):
        cols = slice(t * LANES, (t + 1) * LANES)
        tiles.append(jnp.where(first, piece(2 * t, cols), piece(2 * t + 1, cols)))
    return tiles[0] if len(tiles) == 1 else jnp.concatenate(tiles, axis=1)


def split_blocks(raw, keys, values):
    tokens, lanes = keys.shape
    kinds = 2 * (lanes // LANES)
    size = SPLIT * kinds
    out_row = lax.broadcasted_iota(jnp.int32, (size, size), 0)
    in_row = lax.broadcasted_iota(jnp.int32, (size, size), 1)
    wanted = (out_row % SPLIT) * kinds + out_row // SPLIT
    order = jnp.where(in_row == wanted, 1.0, 0.0).astype(jnp.bfloat16)
    for n in range(tokens // SPLIT):
        sorted_rows = jnp.dot(
            order, raw[n * size : (n + 1) * size, :], preferred_element_type=jnp.float32
        ).astype(jnp.bfloat16)
        for t in range(lanes // LANES):
            at = 2 * t * SPLIT
            rows, cols = slice(n * SPLIT, (n + 1) * SPLIT), slice(t * LANES, (t + 1) * LANES)
            keys[rows, cols] = sorted_rows[at : at + SPLIT]
            values[rows, cols] = sorted_rows[at + SPLIT : at + 2 * SPLIT]


def kernel(
    req_size, tp_size, steps,
    place_ref, owned_ref, plen_ref, table_any, len_any, parents_any,
    q_any, new_any, res_any, gain_any, home_any, prompt_any, wo_any, wq_any,
    qkv_out, res_out,
    table_ref, len_ref, parents_ref,
    q_ref, new_raw, res_ref, gain_ref, home_raw, prompt_raw, wo, wq,
    meta_c, meta_p, qa, qa_msg, qa_in, qb, qb_msg, qb_in, ra, ra_msg, ra_in, rb, rb_msg, rb_in, obuf,
    nk, nv, hk, hv, pk, pv, base, acc,
    load_sem, osend, orecv, *hop_sems
):
    rows, lanes = q_ref.shape
    heads = lanes // HEAD_DIM
    depth = res_ref.shape[1]
    chunk = depth // OUT_CHUNKS
    tokens = hk.shape[0]
    block_count = table_ref.shape[0]
    block = tokens // block_count
    outer, inner = grid_of(req_size)
    planes = 2 * inner
    me = lax.axis_index("req")
    my_tp = lax.axis_index("tp")
    o = me // planes
    p = lax.rem(me, planes)

    half = rows // 2
    mesh_id = pl.DeviceIdType.MESH
    column = (outer, o, lambda n: n * planes + p)
    plane = (planes, p, lambda n: o * planes + n)

    def others(group):
        size, mine, _ = group
        return [lax.rem(mine + d, size) for d in range(1, size)]

    sem_pairs = [hop_sems[n : n + 2] for n in range(0, len(hop_sems), 2)]
    meta_c_sem, meta_p_sem, qa_sem, qa2_sem, qb_sem, qb2_sem, ra_sem, ra2_sem, rb_sem, rb2_sem = sem_pairs
    tp_peers = [lax.rem(my_tp + d, tp_size) for d in range(1, tp_size)]

    barrier = pltpu.get_barrier_semaphore()
    for group in (column, plane):
        for n in others(group):
            pl.semaphore_signal(barrier, inc=1, device_id={"req": group[2](n)}, device_id_type=mesh_id)
    for peer in tp_peers:
        pl.semaphore_signal(barrier, inc=1, device_id={"tp": peer}, device_id_type=mesh_id)

    pairs = [
        (q_any, q_ref), (table_any, table_ref), (len_any, len_ref), (parents_any, parents_ref),
        (prompt_any, prompt_raw), (home_any, home_raw), (new_any, new_raw),
        (wo_any, wo), (res_any, res_ref), (gain_any, gain_ref), (wq_any, wq),
    ]
    loads = [pltpu.make_async_copy(src, dst, load_sem.at[n]) for n, (src, dst) in enumerate(pairs)]
    for copy in loads:
        copy.start()
    sent = []

    def push(src, dst, send_sem, recv_sem, axis, peer):
        copy = pltpu.make_async_remote_copy(
            src_ref=src, dst_ref=dst, send_sem=send_sem, recv_sem=recv_sem,
            device_id={axis: peer}, device_id_type=mesh_id,
        )
        copy.start()
        sent.append(copy)

    def arrive(dst, send_sem, recv_sem, axis, peer):
        pltpu.make_async_remote_copy(
            src_ref=dst, dst_ref=dst, send_sem=send_sem, recv_sem=recv_sem,
            device_id={axis: peer}, device_id_type=mesh_id,
        ).wait_recv()

    def first_hop(buf, group, sems):
        _, mine, index = group
        for d, n in enumerate(others(group)):
            push(buf.at[mine], buf.at[mine], sems[0].at[d], sems[1].at[mine], "req", index(n))

    def wait_hop(buf, group, sems):
        for n in others(group):
            arrive(buf.at[n], sems[0].at[0], sems[1].at[n], "req", group[2](n))

    def second_hop(buf, marks, msg, landed, group, sems):
        held = [buf[s].astype(jnp.float32) for s in range(buf.shape[0])]
        _, mine, index = group

        def chosen(target):
            value = held[0]
            for s in range(1, len(held)):
                value = jnp.where(marks[s] == target.astype(jnp.float32), held[s], value)
            return value.astype(jnp.bfloat16)

        for d, n in enumerate(others(group)):
            msg[d] = chosen(index(n))
            push(msg.at[d], landed.at[mine], sems[0].at[d], sems[1].at[mine], "req", index(n))
        landed[mine] = chosen(me)

    def key_counts():
        lane = lax.broadcasted_iota(jnp.int32, (1, tokens), 1)
        lane_block = lane // block
        lane_pos = lane - lane_block * block
        for b in range(BEAMS):
            total = jnp.zeros((1, tokens), jnp.float32)
            for j in range(block_count):
                live = (lane_block == table_ref[j, b]) & (lane_pos + j * block < len_ref[b])
                total = total + jnp.where(live, 1.0, 0.0)
            base[b : b + 1, :] = total
        pool = base[...]
        row8 = lax.broadcasted_iota(jnp.int32, (BEAMS, BEAMS), 0)
        col8 = lax.broadcasted_iota(jnp.int32, (BEAMS, BEAMS), 1)
        new_row = lax.broadcasted_iota(jnp.int32, (BEAMS, rows), 0)
        new_col = lax.broadcasted_iota(jnp.int32, (BEAMS, rows), 1)
        new = jnp.zeros((BEAMS, rows), jnp.float32)
        pools, news = [], []
        for s in range(steps):
            pick = jnp.zeros((BEAMS, BEAMS), jnp.float32)
            for b in range(BEAMS):
                pick = jnp.where((row8 == b) & (col8 == parents_ref[s, b]), 1.0, pick)
            pool = jnp.dot(pick, pool, preferred_element_type=jnp.float32)
            new = jnp.dot(pick, new, preferred_element_type=jnp.float32)
            new = new + jnp.where(new_col == new_row + s * BEAMS, 1.0, 0.0)
            pools.append(pool)
            news.append(new)
        return jnp.concatenate(pools, axis=0), jnp.concatenate(news, axis=0)

    for copy in loads[:4]:
        copy.wait()
    meta_lane = lax.broadcasted_iota(jnp.int32, (16, LANES), 1)
    mark = (
        jnp.where(meta_lane < LANES // 2, place_ref[0], owned_ref[0])
        .astype(jnp.float32)
        .astype(jnp.bfloat16)
    )
    meta_c[o] = mark
    meta_p[p] = mark
    qa[o] = q_ref[:half, :]
    qb[p] = q_ref[half:, :]
    pl.semaphore_wait(barrier, outer - 1 + planes - 1 + len(tp_peers))
    first_hop(meta_p, plane, meta_p_sem)
    first_hop(qb, plane, qb_sem)
    first_hop(meta_c, column, meta_c_sem)
    first_hop(qa, column, qa_sem)
    loads[4].wait()
    split_blocks(prompt_raw, pk, pv)

    def marks_of(meta):
        rows_of = [meta[s].astype(jnp.float32) for s in range(meta.shape[0])]
        middle = LANES // 2
        return [r[0:1, 0:1] for r in rows_of], [r[0:1, middle : middle + 1] for r in rows_of]

    wait_hop(meta_p, plane, meta_p_sem)
    places_p, owners_p = marks_of(meta_p)
    wait_hop(qb, plane, qb_sem)
    second_hop(qb, places_p, qb_msg, qb_in, column, qb2_sem)
    wait_hop(meta_c, column, meta_c_sem)
    places_c, owners_c = marks_of(meta_c)
    wait_hop(qa, column, qa_sem)
    second_hop(qa, places_c, qa_msg, qa_in, plane, qa2_sem)
    loads[5].wait()
    loads[6].wait()
    split_blocks(home_raw, hk, hv)
    split_blocks(new_raw, nk, nv)
    wait_hop(qa_in, plane, qa2_sem)
    wait_hop(qb_in, column, qb2_sem)

    stat_lane = lax.broadcasted_iota(jnp.int32, (rows, LANES), 1)
    head_lane = stat_lane < heads

    def by_lane(values):
        packed = jnp.zeros((rows, LANES), jnp.float32)
        for h in range(heads):
            packed = jnp.where(stat_lane == h, values[h * rows : (h + 1) * rows], packed)
        return packed

    owned = owned_ref[0]
    asked = jnp.concatenate([qa_in[lax.rem(owned, planes)], qb_in[owned // planes]], axis=0)
    asked = spread_heads(asked, heads)
    scores = dot_t(asked, pk[...])
    prompt_lane = lax.broadcasted_iota(jnp.int32, scores.shape, 1)
    scores = jnp.where(prompt_lane < plen_ref[0], scores, NEG_FILL)
    top = jnp.max(scores, axis=1, keepdims=True)
    weights = jnp.exp(scores - top).astype(jnp.bfloat16)
    total = jnp.sum(weights.astype(jnp.float32), axis=1, keepdims=True)
    wide = jnp.dot(weights, pv[...], preferred_element_type=jnp.float32)
    total = by_lane(total)
    part_of = 1.0 / total
    rest = by_lane(top) + jnp.where(head_lane, jnp.log(total), 0.0)
    stats = jnp.zeros((rows, LANES), jnp.float32)
    for part in range(3):
        level = rest.astype(jnp.bfloat16).astype(jnp.float32)
        rest = rest - level
        stats = stats + (pltpu.roll(level, part * heads, 1) if part else level)

    def answer(h, cols):
        own = slice(h * rows, (h + 1) * rows)
        return wide[own, cols] * part_of[:, h : h + 1]

    answers = own_columns(rows, lanes, answer).astype(jnp.bfloat16)
    stats = stats.astype(jnp.bfloat16)
    rb[p, :, :lanes] = answers[half:]
    rb[p, :, lanes:] = stats[half:]
    ra[o, :, :lanes] = answers[:half]
    ra[o, :, lanes:] = stats[:half]
    first_hop(rb, plane, rb_sem)
    first_hop(ra, column, ra_sem)
    pool_count, new_count = key_counts()

    wait_hop(rb, plane, rb_sem)
    second_hop(rb, owners_p, rb_msg, rb_in, column, rb2_sem)
    query = spread_heads(q_ref[...], heads)
    pool_c = jnp.concatenate([pool_count] * heads, axis=0)
    new_c = jnp.concatenate([new_count] * heads, axis=0)
    pool_s = jnp.where(pool_c > 0.0, dot_t(query, hk[...]), NEG_FILL)
    new_s = jnp.where(new_c > 0.0, dot_t(query, nk[...]), NEG_FILL)
    home_top = jnp.maximum(
        jnp.max(pool_s, axis=1, keepdims=True), jnp.max(new_s, axis=1, keepdims=True)
    )
    pool_w = jnp.exp(pool_s - home_top).astype(jnp.bfloat16).astype(jnp.float32) * pool_c
    new_w = jnp.exp(new_s - home_top).astype(jnp.bfloat16)
    home_sum = jnp.sum(pool_w, axis=1, keepdims=True) + jnp.sum(
        new_w.astype(jnp.float32), axis=1, keepdims=True
    )
    numer = jnp.dot(pool_w.astype(jnp.bfloat16), hv[...], preferred_element_type=jnp.float32)
    numer = numer + jnp.dot(new_w, nv[...], preferred_element_type=jnp.float32)

    home_top = by_lane(home_top)
    home_sum = by_lane(home_sum)

    wait_hop(ra, column, ra_sem)
    second_hop(ra, owners_c, ra_msg, ra_in, plane, ra2_sem)
    wait_hop(ra_in, plane, ra2_sem)
    wait_hop(rb_in, column, rb2_sem)
    place = place_ref[0]
    reply = jnp.concatenate([ra_in[lax.rem(place, planes)], rb_in[place // planes]], axis=0)
    reply = reply.astype(jnp.float32)
    stats = reply[:, lanes:]
    reply_log = stats + pltpu.roll(stats, LANES - heads, 1) + pltpu.roll(stats, LANES - 2 * heads, 1)
    reply_log = jnp.where(head_lane, reply_log, 0.0)
    joint = jnp.maximum(home_top, reply_log)
    home_factor = jnp.exp(home_top - joint)
    prompt_factor = jnp.exp(reply_log - joint)
    scale = 1.0 / (home_sum * home_factor + prompt_factor)
    home_factor = home_factor * scale
    prompt_factor = prompt_factor * scale

    def joined(h, cols):
        own = slice(h * rows, (h + 1) * rows)
        lane = slice(h, h + 1)
        return numer[own, cols] * home_factor[:, lane] + reply[:, cols] * prompt_factor[:, lane]

    attended = own_columns(rows, lanes, joined).astype(jnp.bfloat16)

    loads[7].wait()
    for k in range(OUT_CHUNKS):
        cols = slice(k * chunk, (k + 1) * chunk)
        part = jnp.dot(attended, wo[:, cols], preferred_element_type=jnp.float32)
        obuf[my_tp, k] = part.astype(jnp.bfloat16)
        for d, peer in enumerate(tp_peers):
            mine = obuf.at[my_tp, k]
            push(mine, mine, osend.at[k * len(tp_peers) + d], orecv.at[my_tp, k], "tp", peer)

    for copy in loads[8:]:
        copy.wait()
    gain_all = gain_ref[...].astype(jnp.float32)
    square = jnp.zeros((rows, 1), jnp.float32)
    for k in range(OUT_CHUNKS):
        cols = slice(k * chunk, (k + 1) * chunk)
        for peer in tp_peers:
            arrive(obuf.at[peer, k], osend.at[0], orecv.at[peer, k], "tp", peer)
        summed = obuf[0, k].astype(jnp.float32)
        for t in range(1, tp_size):
            summed = summed + obuf[t, k].astype(jnp.float32)
        mixed = res_ref[:, cols].astype(jnp.float32) + summed
        res_out[:, cols] = mixed.astype(jnp.bfloat16)
        square = square + jnp.sum(mixed * mixed, axis=1, keepdims=True)
        gain_rows = [gain_all[n : n + 1] for n in range(k * chunk // LANES, (k + 1) * chunk // LANES)]
        gained = (mixed * jnp.concatenate(gain_rows, axis=1)).astype(jnp.bfloat16)
        for n in range(3):
            term = jnp.dot(gained, wq[n, cols, :], preferred_element_type=jnp.float32)
            if k == 0:
                acc[n] = term
            else:
                acc[n] += term
    inverse = lax.rsqrt(square / depth + NORM_EPS)
    for n in range(3):
        scaled = acc[n] * inverse
        for s in range(steps):
            qkv_out[s, n] = scaled[s * BEAMS : (s + 1) * BEAMS].astype(jnp.bfloat16)

    for copy in sent:
        copy.wait_send()


def store(qkv_ref, res_ref, qkv_out, res_out, sems):
    copies = [
        pltpu.make_async_copy(qkv_ref, qkv_out, sems.at[0]),
        pltpu.make_async_copy(res_ref, res_out, sems.at[1]),
    ]
    for copy in copies:
        copy.start()
    for copy in copies:
        copy.wait()


def token_rows(cache):
    lanes = cache.shape[-1]
    tiles = cache.reshape(-1, 2, lanes // LANES, LANES).transpose(0, 2, 1, 3)
    return tiles.reshape(-1, LANES)


def shards(
    queries, new_kv, residual, home_cache, prompt_cache, home_table, home_len,
    parents, prompt_place, owned_request, prompt_len, out_weight, norm_gain, qkv_weight,
):
    steps, beams, lanes = queries.shape
    rows = steps * beams
    depth = residual.shape[2]
    req_size = lax.axis_size("req")
    tp_size = lax.axis_size("tp")
    outer, inner = grid_of(req_size)
    planes = 2 * inner
    tokens = home_cache.shape[0] * home_cache.shape[1]
    smem = pl.BlockSpec(memory_space=pltpu.SMEM)
    vmem = pl.BlockSpec(memory_space=pltpu.VMEM)
    hbm = pl.BlockSpec(memory_space=pltpu.HBM)
    bf16, f32 = jnp.bfloat16, jnp.float32
    dma = pltpu.SemaphoreType.DMA
    singles = (prompt_place, owned_request, prompt_len)
    ints = (home_table.T, home_len, parents)
    floats = (
        queries.reshape(rows, lanes),
        token_rows(new_kv),
        residual.reshape(rows, depth),
        norm_gain.reshape(-1, LANES),
        token_rows(home_cache),
        token_rows(prompt_cache),
        out_weight,
        qkv_weight.transpose(1, 0, 2),
    )
    wide = lanes + LANES
    half = rows // 2

    def route(first, second, width):
        return [
            pltpu.VMEM((first, half, width), bf16),
            pltpu.VMEM((second - 1, half, width), bf16),
            pltpu.VMEM((second, half, width), bf16),
        ]

    hops = [outer, planes] + [outer, planes, planes, outer] * 2
    sems = [(len(ints) + len(floats),), (OUT_CHUNKS * tp_size,), (tp_size, OUT_CHUNKS)]
    sems += [(size,) for size in hops for _ in range(2)]
    qkv, res = pl.pallas_call(
        functools.partial(kernel, req_size, tp_size, steps),
        out_shape=(
            jax.ShapeDtypeStruct((steps, 3, beams, lanes), bf16),
            jax.ShapeDtypeStruct((rows, depth), bf16),
        ),
        in_specs=[smem] * len(singles) + [hbm] * (len(ints) + len(floats)),
        out_specs=(vmem, vmem),
        scratch_shapes=[pltpu.SMEM(a.shape, jnp.int32) for a in ints]
        + [pltpu.VMEM(a.shape, bf16) for a in floats]
        + [
            pltpu.VMEM((outer, 16, LANES), bf16),
            pltpu.VMEM((planes, 16, LANES), bf16),
        ]
        + route(outer, planes, lanes)
        + route(planes, outer, lanes)
        + route(outer, planes, wide)
        + route(planes, outer, wide)
        + [
            pltpu.VMEM((tp_size, OUT_CHUNKS, rows, depth // OUT_CHUNKS), bf16),
            pltpu.VMEM((rows, lanes), bf16),
            pltpu.VMEM((rows, lanes), bf16),
            pltpu.VMEM((tokens, lanes), bf16),
            pltpu.VMEM((tokens, lanes), bf16),
            pltpu.VMEM((tokens, lanes), bf16),
            pltpu.VMEM((tokens, lanes), bf16),
            pltpu.VMEM((beams, tokens), f32),
            pltpu.VMEM((3, rows, lanes), f32),
        ]
        + [dma(shape) for shape in sems],
        compiler_params=pltpu.CompilerParams(
            collective_id=0, has_side_effects=True, vmem_limit_bytes=40 * 1024 * 1024
        ),
    )(*singles, *(pltpu.with_memory_space_constraint(x, pltpu.HBM) for x in ints + floats))
    qkv, res = pl.pallas_call(
        store,
        out_shape=(
            jax.ShapeDtypeStruct(qkv.shape, bf16),
            jax.ShapeDtypeStruct(res.shape, bf16),
        ),
        in_specs=[vmem, vmem],
        out_specs=(hbm, hbm),
        scratch_shapes=[dma((2,))],
    )(qkv, res)
    return qkv.transpose(0, 2, 1, 3), res.reshape(steps, beams, depth)


def solution(mesh):
    placed = (
        P(None, "req", "tp"),
        P(None, "req", None, "tp"),
        P(None, "req", None),
        P("req", None, None, "tp"),
        P("req", None, None, "tp"),
        P("req", None),
        P("req"),
        P(None, "req"),
        P("req"),
        P("req"),
        P("req"),
        P("tp", None),
        P(),
        P(None, None, "tp"),
    )
    return jax.shard_map(
        shards,
        mesh=mesh,
        in_specs=placed,
        out_specs=(P(None, "req", None, "tp"), P(None, "req", None)),
        check_vma=False,
    )
```

```python
import functools
import math

import jax
import jax.numpy as jnp
from jax import lax
from jax.experimental import pallas as pl
from jax.experimental.pallas import tpu as pltpu
from jax.sharding import PartitionSpec as P

HEAD_DIM = 64
BEAMS = 8
LANES = 128
OUT_CHUNKS = 4
SPLIT = 32

NEG_FILL = -1e30
NORM_EPS = 1e-05


def grid_of(req_size):
    chips = req_size // 2
    outer = 4 if chips % 4 == 0 else 1
    return outer, chips // outer


def spread_heads(q, heads):
    rows, lanes = q.shape
    scaled = q.astype(jnp.float32) * (1.0 / math.sqrt(HEAD_DIM))
    lane_head = lax.broadcasted_iota(jnp.int32, (rows, lanes), 1) // HEAD_DIM
    parts = [jnp.where(lane_head == h, scaled, 0.0) for h in range(heads)]
    return jnp.concatenate(parts, axis=0).astype(jnp.bfloat16)


def dot_t(a, b):
    return lax.dot_general(a, b, (((1,), (1,)), ((), ())), preferred_element_type=jnp.float32)


def own_columns(rows, lanes, piece):
    first = lax.broadcasted_iota(jnp.int32, (rows, LANES), 1) < HEAD_DIM
    tiles = []
    for t in range(lanes // LANES):
        cols = slice(t * LANES, (t + 1) * LANES)
        tiles.append(jnp.where(first, piece(2 * t, cols), piece(2 * t + 1, cols)))
    return tiles[0] if len(tiles) == 1 else jnp.concatenate(tiles, axis=1)


def split_blocks(raw, keys, values):
    tokens, lanes = keys.shape
    kinds = 2 * (lanes // LANES)
    size = SPLIT * kinds
    out_row = lax.broadcasted_iota(jnp.int32, (size, size), 0)
    in_row = lax.broadcasted_iota(jnp.int32, (size, size), 1)
    wanted = (out_row % SPLIT) * kinds + out_row // SPLIT
    order = jnp.where(in_row == wanted, 1.0, 0.0).astype(jnp.bfloat16)
    for n in range(tokens // SPLIT):
        sorted_rows = jnp.dot(
            order, raw[n * size : (n + 1) * size, :], preferred_element_type=jnp.float32
        ).astype(jnp.bfloat16)
        for t in range(lanes // LANES):
            at = 2 * t * SPLIT
            rows, cols = slice(n * SPLIT, (n + 1) * SPLIT), slice(t * LANES, (t + 1) * LANES)
            keys[rows, cols] = sorted_rows[at : at + SPLIT]
            values[rows, cols] = sorted_rows[at + SPLIT : at + 2 * SPLIT]


def kernel(
    req_size, tp_size, steps,
    place_ref, owned_ref, plen_ref, table_any, len_any, parents_any,
    q_any, new_any, res_any, gain_any, home_any, prompt_any, wo_any, wq_any,
    qkv_out, res_out,
    table_ref, len_ref, parents_ref,
    q_ref, new_raw, res_ref, gain_ref, home_raw, prompt_raw, wo, wq,
    meta_c, meta_p, qa, qa_msg, qa_in, qb, qb_msg, qb_in, ra, ra_msg, ra_in, rb, rb_msg, rb_in, obuf,
    nk, nv, hk, hv, pk, pv, base, acc,
    load_sem, osend, orecv, *hop_sems
):
    rows, lanes = q_ref.shape
    heads = lanes // HEAD_DIM
    depth = res_ref.shape[1]
    chunk = depth // OUT_CHUNKS
    tokens = hk.shape[0]
    block_count = table_ref.shape[0]
    block = tokens // block_count
    outer, inner = grid_of(req_size)
    planes = 2 * inner
    me = lax.axis_index("req")
    my_tp = lax.axis_index("tp")
    o = me // planes
    p = lax.rem(me, planes)

    half = rows // 2
    mesh_id = pl.DeviceIdType.MESH
    column = (outer, o, lambda n: n * planes + p)
    plane = (planes, p, lambda n: o * planes + n)

    def others(group):
        size, mine, _ = group
        return [lax.rem(mine + d, size) for d in range(1, size)]

    sem_pairs = [hop_sems[n : n + 2] for n in range(0, len(hop_sems), 2)]
    meta_c_sem, meta_p_sem, qa_sem, qa2_sem, qb_sem, qb2_sem, ra_sem, ra2_sem, rb_sem, rb2_sem = sem_pairs
    tp_peers = [lax.rem(my_tp + d, tp_size) for d in range(1, tp_size)]

    barrier = pltpu.get_barrier_semaphore()
    for group in (column, plane):
        for n in others(group):
            pl.semaphore_signal(barrier, inc=1, device_id={"req": group[2](n)}, device_id_type=mesh_id)
    for peer in tp_peers:
        pl.semaphore_signal(barrier, inc=1, device_id={"tp": peer}, device_id_type=mesh_id)

    pairs = [
        (q_any, q_ref), (table_any, table_ref), (len_any, len_ref), (parents_any, parents_ref),
        (prompt_any, prompt_raw), (home_any, home_raw), (new_any, new_raw),
        (wo_any, wo), (res_any, res_ref), (gain_any, gain_ref), (wq_any, wq),
    ]
    loads = [pltpu.make_async_copy(src, dst, load_sem.at[n]) for n, (src, dst) in enumerate(pairs)]
    for copy in loads[:5]:
        copy.start()
    sent = []

    def push(src, dst, send_sem, recv_sem, axis, peer):
        copy = pltpu.make_async_remote_copy(
            src_ref=src, dst_ref=dst, send_sem=send_sem, recv_sem=recv_sem,
            device_id={axis: peer}, device_id_type=mesh_id,
        )
        copy.start()
        sent.append(copy)

    def arrive(dst, send_sem, recv_sem, axis, peer):
        pltpu.make_async_remote_copy(
            src_ref=dst, dst_ref=dst, send_sem=send_sem, recv_sem=recv_sem,
            device_id={axis: peer}, device_id_type=mesh_id,
        ).wait_recv()

    def first_hop(buf, group, sems):
        _, mine, index = group
        for d, n in enumerate(others(group)):
            push(buf.at[mine], buf.at[mine], sems[0].at[d], sems[1].at[mine], "req", index(n))

    def wait_hop(buf, group, sems):
        for n in others(group):
            arrive(buf.at[n], sems[0].at[0], sems[1].at[n], "req", group[2](n))

    def second_hop(buf, marks, msg, landed, group, sems):
        held = [buf[s].astype(jnp.float32) for s in range(buf.shape[0])]
        _, mine, index = group

        def chosen(target):
            value = held[0]
            for s in range(1, len(held)):
                value = jnp.where(marks[s] == target.astype(jnp.float32), held[s], value)
            return value.astype(jnp.bfloat16)

        for d, n in enumerate(others(group)):
            msg[d] = chosen(index(n))
            push(msg.at[d], landed.at[mine], sems[0].at[d], sems[1].at[mine], "req", index(n))
        landed[mine] = chosen(me)

    def key_counts():
        lane = lax.broadcasted_iota(jnp.int32, (1, tokens), 1)
        lane_block = lane // block
        lane_pos = lane - lane_block * block
        for b in range(BEAMS):
            total = jnp.zeros((1, tokens), jnp.float32)
            for j in range(block_count):
                live = (lane_block == table_ref[j, b]) & (lane_pos + j * block < len_ref[b])
                total = total + jnp.where(live, 1.0, 0.0)
            base[b : b + 1, :] = total
        pool = base[...]
        row8 = lax.broadcasted_iota(jnp.int32, (BEAMS, BEAMS), 0)
        col8 = lax.broadcasted_iota(jnp.int32, (BEAMS, BEAMS), 1)
        new_row = lax.broadcasted_iota(jnp.int32, (BEAMS, rows), 0)
        new_col = lax.broadcasted_iota(jnp.int32, (BEAMS, rows), 1)
        new = jnp.zeros((BEAMS, rows), jnp.float32)
        pools, news = [], []
        for s in range(steps):
            pick = jnp.zeros((BEAMS, BEAMS), jnp.float32)
            for b in range(BEAMS):
                pick = jnp.where((row8 == b) & (col8 == parents_ref[s, b]), 1.0, pick)
            pool = jnp.dot(pick, pool, preferred_element_type=jnp.float32)
            new = jnp.dot(pick, new, preferred_element_type=jnp.float32)
            new = new + jnp.where(new_col == new_row + s * BEAMS, 1.0, 0.0)
            pools.append(pool)
            news.append(new)
        return jnp.concatenate(pools, axis=0), jnp.concatenate(news, axis=0)

    for copy in loads[:4]:
        copy.wait()
    meta_lane = lax.broadcasted_iota(jnp.int32, (16, LANES), 1)
    mark = (
        jnp.where(meta_lane < LANES // 2, place_ref[0], owned_ref[0])
        .astype(jnp.float32)
        .astype(jnp.bfloat16)
    )
    meta_c[o] = mark
    meta_p[p] = mark
    qa[o] = q_ref[:half, :]
    qb[p] = q_ref[half:, :]
    pl.semaphore_wait(barrier, outer - 1 + planes - 1 + len(tp_peers))
    first_hop(qa, column, qa_sem)
    first_hop(qb, plane, qb_sem)
    first_hop(meta_p, plane, meta_p_sem)
    first_hop(meta_c, column, meta_c_sem)
    loads[5].start()
    loads[6].start()
    loads[4].wait()
    split_blocks(prompt_raw, pk, pv)

    def marks_of(meta):
        rows_of = [meta[s].astype(jnp.float32) for s in range(meta.shape[0])]
        middle = LANES // 2
        return [r[0:1, 0:1] for r in rows_of], [r[0:1, middle : middle + 1] for r in rows_of]

    wait_hop(meta_p, plane, meta_p_sem)
    places_p, owners_p = marks_of(meta_p)
    wait_hop(qb, plane, qb_sem)
    second_hop(qb, places_p, qb_msg, qb_in, column, qb2_sem)
    wait_hop(meta_c, column, meta_c_sem)
    places_c, owners_c = marks_of(meta_c)
    wait_hop(qa, column, qa_sem)
    second_hop(qa, places_c, qa_msg, qa_in, plane, qa2_sem)
    for copy in loads[7:]:
        copy.start()
    loads[5].wait()
    loads[6].wait()
    split_blocks(home_raw, hk, hv)
    split_blocks(new_raw, nk, nv)
    wait_hop(qa_in, plane, qa2_sem)
    wait_hop(qb_in, column, qb2_sem)

    stat_lane = lax.broadcasted_iota(jnp.int32, (rows, LANES), 1)
    head_lane = stat_lane < heads

    def by_lane(values):
        packed = jnp.zeros((rows, LANES), jnp.float32)
        for h in range(heads):
            packed = jnp.where(stat_lane == h, values[h * rows : (h + 1) * rows], packed)
        return packed

    owned = owned_ref[0]
    asked = jnp.concatenate([qa_in[lax.rem(owned, planes)], qb_in[owned // planes]], axis=0)
    asked = spread_heads(asked, heads)
    scores = dot_t(asked, pk[...])
    prompt_lane = lax.broadcasted_iota(jnp.int32, scores.shape, 1)
    scores = jnp.where(prompt_lane < plen_ref[0], scores, NEG_FILL)
    top = jnp.max(scores, axis=1, keepdims=True)
    weights = jnp.exp(scores - top).astype(jnp.bfloat16)
    total = jnp.sum(weights.astype(jnp.float32), axis=1, keepdims=True)
    wide = jnp.dot(weights, pv[...], preferred_element_type=jnp.float32)
    total = by_lane(total)
    part_of = 1.0 / total
    rest = by_lane(top) + jnp.where(head_lane, jnp.log(total), 0.0)
    stats = jnp.zeros((rows, LANES), jnp.float32)
    for part in range(3):
        level = rest.astype(jnp.bfloat16).astype(jnp.float32)
        rest = rest - level
        stats = stats + (pltpu.roll(level, part * heads, 1) if part else level)

    def answer(h, cols):
        own = slice(h * rows, (h + 1) * rows)
        return wide[own, cols] * part_of[:, h : h + 1]

    answers = own_columns(rows, lanes, answer).astype(jnp.bfloat16)
    stats = stats.astype(jnp.bfloat16)
    ra[o, :, :lanes] = answers[:half]
    ra[o, :, lanes:] = stats[:half]
    rb[p, :, :lanes] = answers[half:]
    rb[p, :, lanes:] = stats[half:]
    first_hop(ra, column, ra_sem)
    first_hop(rb, plane, rb_sem)
    pool_count, new_count = key_counts()

    wait_hop(rb, plane, rb_sem)
    second_hop(rb, owners_p, rb_msg, rb_in, column, rb2_sem)
    query = spread_heads(q_ref[...], heads)
    pool_c = jnp.concatenate([pool_count] * heads, axis=0)
    new_c = jnp.concatenate([new_count] * heads, axis=0)
    pool_s = jnp.where(pool_c > 0.0, dot_t(query, hk[...]), NEG_FILL)
    new_s = jnp.where(new_c > 0.0, dot_t(query, nk[...]), NEG_FILL)
    home_top = jnp.maximum(
        jnp.max(pool_s, axis=1, keepdims=True), jnp.max(new_s, axis=1, keepdims=True)
    )
    pool_w = jnp.exp(pool_s - home_top).astype(jnp.bfloat16).astype(jnp.float32) * pool_c
    new_w = jnp.exp(new_s - home_top).astype(jnp.bfloat16)
    home_sum = jnp.sum(pool_w, axis=1, keepdims=True) + jnp.sum(
        new_w.astype(jnp.float32), axis=1, keepdims=True
    )
    numer = jnp.dot(pool_w.astype(jnp.bfloat16), hv[...], preferred_element_type=jnp.float32)
    numer = numer + jnp.dot(new_w, nv[...], preferred_element_type=jnp.float32)

    home_top = by_lane(home_top)
    home_sum = by_lane(home_sum)

    wait_hop(ra, column, ra_sem)
    second_hop(ra, owners_c, ra_msg, ra_in, plane, ra2_sem)
    wait_hop(ra_in, plane, ra2_sem)
    wait_hop(rb_in, column, rb2_sem)
    place = place_ref[0]
    reply = jnp.concatenate([ra_in[lax.rem(place, planes)], rb_in[place // planes]], axis=0)
    reply = reply.astype(jnp.float32)
    stats = reply[:, lanes:]
    reply_log = stats + pltpu.roll(stats, LANES - heads, 1) + pltpu.roll(stats, LANES - 2 * heads, 1)
    reply_log = jnp.where(head_lane, reply_log, 0.0)
    joint = jnp.maximum(home_top, reply_log)
    home_factor = jnp.exp(home_top - joint)
    prompt_factor = jnp.exp(reply_log - joint)
    scale = 1.0 / (home_sum * home_factor + prompt_factor)
    home_factor = home_factor * scale
    prompt_factor = prompt_factor * scale

    def joined(h, cols):
        own = slice(h * rows, (h + 1) * rows)
        lane = slice(h, h + 1)
        return numer[own, cols] * home_factor[:, lane] + reply[:, cols] * prompt_factor[:, lane]

    attended = own_columns(rows, lanes, joined).astype(jnp.bfloat16)

    loads[7].wait()
    for k in range(OUT_CHUNKS):
        cols = slice(k * chunk, (k + 1) * chunk)
        part = jnp.dot(attended, wo[:, cols], preferred_element_type=jnp.float32)
        obuf[my_tp, k] = part.astype(jnp.bfloat16)
        for d, peer in enumerate(tp_peers):
            mine = obuf.at[my_tp, k]
            push(mine, mine, osend.at[k * len(tp_peers) + d], orecv.at[my_tp, k], "tp", peer)

    for copy in loads[8:]:
        copy.wait()
    gain_all = gain_ref[...].astype(jnp.float32)
    square = jnp.zeros((rows, 1), jnp.float32)
    for k in range(OUT_CHUNKS):
        cols = slice(k * chunk, (k + 1) * chunk)
        for peer in tp_peers:
            arrive(obuf.at[peer, k], osend.at[0], orecv.at[peer, k], "tp", peer)
        summed = obuf[0, k].astype(jnp.float32)
        for t in range(1, tp_size):
            summed = summed + obuf[t, k].astype(jnp.float32)
        mixed = res_ref[:, cols].astype(jnp.float32) + summed
        res_out[:, cols] = mixed.astype(jnp.bfloat16)
        square = square + jnp.sum(mixed * mixed, axis=1, keepdims=True)
        gain_rows = [gain_all[n : n + 1] for n in range(k * chunk // LANES, (k + 1) * chunk // LANES)]
        gained = (mixed * jnp.concatenate(gain_rows, axis=1)).astype(jnp.bfloat16)
        for n in range(3):
            term = jnp.dot(gained, wq[n, cols, :], preferred_element_type=jnp.float32)
            if k == 0:
                acc[n] = term
            else:
                acc[n] += term
    inverse = lax.rsqrt(square / depth + NORM_EPS)
    for n in range(3):
        scaled = acc[n] * inverse
        for s in range(steps):
            qkv_out[s, n] = scaled[s * BEAMS : (s + 1) * BEAMS].astype(jnp.bfloat16)

    for copy in sent:
        copy.wait_send()


def token_rows(cache):
    lanes = cache.shape[-1]
    tiles = cache.reshape(-1, 2, lanes // LANES, LANES).transpose(0, 2, 1, 3)
    return tiles.reshape(-1, LANES)


def shards(
    queries, new_kv, residual, home_cache, prompt_cache, home_table, home_len,
    parents, prompt_place, owned_request, prompt_len, out_weight, norm_gain, qkv_weight,
):
    steps, beams, lanes = queries.shape
    rows = steps * beams
    depth = residual.shape[2]
    req_size = lax.axis_size("req")
    tp_size = lax.axis_size("tp")
    outer, inner = grid_of(req_size)
    planes = 2 * inner
    tokens = home_cache.shape[0] * home_cache.shape[1]
    smem = pl.BlockSpec(memory_space=pltpu.SMEM)
    vmem = pl.BlockSpec(memory_space=pltpu.VMEM)
    hbm = pl.BlockSpec(memory_space=pltpu.HBM)
    bf16, f32 = jnp.bfloat16, jnp.float32
    dma = pltpu.SemaphoreType.DMA
    singles = (prompt_place, owned_request, prompt_len)
    ints = (home_table.T, home_len, parents)
    floats = (
        queries.reshape(rows, lanes),
        token_rows(new_kv),
        residual.reshape(rows, depth),
        norm_gain.reshape(-1, LANES),
        token_rows(home_cache),
        token_rows(prompt_cache),
        out_weight,
        qkv_weight.transpose(1, 0, 2),
    )
    wide = lanes + LANES
    half = rows // 2

    def route(first, second, width):
        return [
            pltpu.VMEM((first, half, width), bf16),
            pltpu.VMEM((second - 1, half, width), bf16),
            pltpu.VMEM((second, half, width), bf16),
        ]

    hops = [outer, planes] + [outer, planes, planes, outer] * 2
    sems = [(len(ints) + len(floats),), (OUT_CHUNKS * tp_size,), (tp_size, OUT_CHUNKS)]
    sems += [(size,) for size in hops for _ in range(2)]
    qkv, res = pl.pallas_call(
        functools.partial(kernel, req_size, tp_size, steps),
        out_shape=(
            jax.ShapeDtypeStruct((steps, 3, beams, lanes), bf16),
            jax.ShapeDtypeStruct((rows, depth), bf16),
        ),
        in_specs=[smem] * len(singles) + [hbm] * (len(ints) + len(floats)),
        out_specs=(vmem, vmem),
        scratch_shapes=[pltpu.SMEM(a.shape, jnp.int32) for a in ints]
        + [pltpu.VMEM(a.shape, bf16) for a in floats]
        + [
            pltpu.VMEM((outer, 16, LANES), bf16),
            pltpu.VMEM((planes, 16, LANES), bf16),
        ]
        + route(outer, planes, lanes)
        + route(planes, outer, lanes)
        + route(outer, planes, wide)
        + route(planes, outer, wide)
        + [
            pltpu.VMEM((tp_size, OUT_CHUNKS, rows, depth // OUT_CHUNKS), bf16),
            pltpu.VMEM((rows, lanes), bf16),
            pltpu.VMEM((rows, lanes), bf16),
            pltpu.VMEM((tokens, lanes), bf16),
            pltpu.VMEM((tokens, lanes), bf16),
            pltpu.VMEM((tokens, lanes), bf16),
            pltpu.VMEM((tokens, lanes), bf16),
            pltpu.VMEM((beams, tokens), f32),
            pltpu.VMEM((3, rows, lanes), f32),
        ]
        + [dma(shape) for shape in sems],
        compiler_params=pltpu.CompilerParams(
            collective_id=0, has_side_effects=True, vmem_limit_bytes=40 * 1024 * 1024
        ),
    )(*singles, *(pltpu.with_memory_space_constraint(x, pltpu.HBM) for x in ints + floats))
    return qkv.transpose(0, 2, 1, 3), res.reshape(steps, beams, depth)


def solution(mesh):
    placed = (
        P(None, "req", "tp"),
        P(None, "req", None, "tp"),
        P(None, "req", None),
        P("req", None, None, "tp"),
        P("req", None, None, "tp"),
        P("req", None),
        P("req"),
        P(None, "req"),
        P("req"),
        P("req"),
        P("req"),
        P("tp", None),
        P(),
        P(None, None, "tp"),
    )
    return jax.shard_map(
        shards,
        mesh=mesh,
        in_specs=placed,
        out_specs=(P(None, "req", None, "tp"), P(None, "req", None)),
        check_vma=False,
    )
```

```python
import functools
import math

import jax
import jax.numpy as jnp
from jax import lax
from jax.experimental import pallas as pl
from jax.experimental.pallas import tpu as pltpu
from jax.sharding import PartitionSpec as P

HEAD_DIM = 64
BEAMS = 8
LANES = 128
OUT_CHUNKS = 4
SPLIT = 32

NEG_FILL = -1e30
NORM_EPS = 1e-05


def grid_of(req_size):
    chips = req_size // 2
    outer = 4 if chips % 4 == 0 else 1
    return outer, chips // outer


def spread_heads(q, heads):
    rows, lanes = q.shape
    scaled = q.astype(jnp.float32) * (1.0 / math.sqrt(HEAD_DIM))
    lane_head = lax.broadcasted_iota(jnp.int32, (rows, lanes), 1) // HEAD_DIM
    parts = [jnp.where(lane_head == h, scaled, 0.0) for h in range(heads)]
    return jnp.concatenate(parts, axis=0).astype(jnp.bfloat16)


def dot_t(a, b):
    return lax.dot_general(a, b, (((1,), (1,)), ((), ())), preferred_element_type=jnp.float32)


def own_columns(rows, lanes, piece):
    first = lax.broadcasted_iota(jnp.int32, (rows, LANES), 1) < HEAD_DIM
    tiles = []
    for t in range(lanes // LANES):
        cols = slice(t * LANES, (t + 1) * LANES)
        tiles.append(jnp.where(first, piece(2 * t, cols), piece(2 * t + 1, cols)))
    return tiles[0] if len(tiles) == 1 else jnp.concatenate(tiles, axis=1)


def split_blocks(raw, keys, values):
    tokens, lanes = keys.shape
    kinds = 2 * (lanes // LANES)
    size = SPLIT * kinds
    out_row = lax.broadcasted_iota(jnp.int32, (size, size), 0)
    in_row = lax.broadcasted_iota(jnp.int32, (size, size), 1)
    wanted = (out_row % SPLIT) * kinds + out_row // SPLIT
    order = jnp.where(in_row == wanted, 1.0, 0.0).astype(jnp.bfloat16)
    blocks = tokens // SPLIT
    group = min(4, blocks)
    for first in range(0, blocks, group):
        taken = range(first, first + group)
        beside = [raw[n * size : (n + 1) * size, :] for n in taken]
        beside = beside[0] if group == 1 else jnp.concatenate(beside, axis=1)
        ordered = jnp.dot(order, beside, preferred_element_type=jnp.float32).astype(jnp.bfloat16)
        for g, n in enumerate(taken):
            rows, own = slice(n * SPLIT, (n + 1) * SPLIT), slice(g * LANES, (g + 1) * LANES)
            for t in range(lanes // LANES):
                at = 2 * t * SPLIT
                cols = slice(t * LANES, (t + 1) * LANES)
                keys[rows, cols] = ordered[at : at + SPLIT, own]
                values[rows, cols] = ordered[at + SPLIT : at + 2 * SPLIT, own]


def kernel(
    req_size, tp_size, steps,
    place_ref, owned_ref, plen_ref, table_any, len_any, parents_any,
    q_any, new_any, res_any, gain_any, home_any, prompt_any, wo_any, wq_any,
    qkv_out, res_out,
    table_ref, len_ref, parents_ref,
    q_ref, new_raw, res_ref, gain_ref, home_raw, prompt_raw, wo, wq,
    meta_c, meta_p, qa, qa_msg, qa_in, qb, qb_msg, qb_in, ra, ra_msg, ra_in, rb, rb_msg, rb_in, obuf,
    nk, nv, hk, hv, pk, pv, base, acc,
    load_sem, osend, orecv, *hop_sems
):
    rows, lanes = q_ref.shape
    heads = lanes // HEAD_DIM
    depth = res_ref.shape[1]
    chunk = depth // OUT_CHUNKS
    tokens = hk.shape[0]
    block_count = table_ref.shape[0]
    block = tokens // block_count
    outer, inner = grid_of(req_size)
    planes = 2 * inner
    me = lax.axis_index("req")
    my_tp = lax.axis_index("tp")
    o = me // planes
    p = lax.rem(me, planes)

    half = rows // 2
    mesh_id = pl.DeviceIdType.MESH
    column = (outer, o, lambda n: n * planes + p)
    plane = (planes, p, lambda n: o * planes + n)

    def others(group):
        size, mine, _ = group
        return [lax.rem(mine + d, size) for d in range(1, size)]

    sem_pairs = [hop_sems[n : n + 2] for n in range(0, len(hop_sems), 2)]
    meta_c_sem, meta_p_sem, qa_sem, qa2_sem, qb_sem, qb2_sem, ra_sem, ra2_sem, rb_sem, rb2_sem = sem_pairs
    tp_peers = [lax.rem(my_tp + d, tp_size) for d in range(1, tp_size)]

    barrier = pltpu.get_barrier_semaphore()
    for group in (column, plane):
        for n in others(group):
            pl.semaphore_signal(barrier, inc=1, device_id={"req": group[2](n)}, device_id_type=mesh_id)
    for peer in tp_peers:
        pl.semaphore_signal(barrier, inc=1, device_id={"tp": peer}, device_id_type=mesh_id)

    pairs = [
        (q_any, q_ref), (table_any, table_ref), (len_any, len_ref), (parents_any, parents_ref),
        (prompt_any, prompt_raw), (home_any, home_raw), (new_any, new_raw),
        (wo_any, wo), (res_any, res_ref), (gain_any, gain_ref), (wq_any, wq),
    ]
    loads = [pltpu.make_async_copy(src, dst, load_sem.at[n]) for n, (src, dst) in enumerate(pairs)]
    for copy in loads[:5]:
        copy.start()
    sent = []

    def push(src, dst, send_sem, recv_sem, axis, peer):
        copy = pltpu.make_async_remote_copy(
            src_ref=src, dst_ref=dst, send_sem=send_sem, recv_sem=recv_sem,
            device_id={axis: peer}, device_id_type=mesh_id,
        )
        copy.start()
        sent.append(copy)

    def arrive(dst, send_sem, recv_sem, axis, peer):
        pltpu.make_async_remote_copy(
            src_ref=dst, dst_ref=dst, send_sem=send_sem, recv_sem=recv_sem,
            device_id={axis: peer}, device_id_type=mesh_id,
        ).wait_recv()

    def first_hop(buf, group, sems):
        _, mine, index = group
        for d, n in enumerate(others(group)):
            push(buf.at[mine], buf.at[mine], sems[0].at[d], sems[1].at[mine], "req", index(n))

    def wait_hop(buf, group, sems):
        for n in others(group):
            arrive(buf.at[n], sems[0].at[0], sems[1].at[n], "req", group[2](n))

    def second_hop(buf, marks, msg, landed, group, sems):
        held = [buf[s].astype(jnp.float32) for s in range(buf.shape[0])]
        _, mine, index = group

        def chosen(target):
            value = held[0]
            for s in range(1, len(held)):
                value = jnp.where(marks[s] == target.astype(jnp.float32), held[s], value)
            return value.astype(jnp.bfloat16)

        for d, n in enumerate(others(group)):
            msg[d] = chosen(index(n))
            push(msg.at[d], landed.at[mine], sems[0].at[d], sems[1].at[mine], "req", index(n))
        landed[mine] = chosen(me)

    def key_counts():
        lane = lax.broadcasted_iota(jnp.int32, (1, tokens), 1)
        lane_block = lane // block
        lane_pos = lane - lane_block * block
        for b in range(BEAMS):
            total = jnp.zeros((1, tokens), jnp.float32)
            for j in range(block_count):
                live = (lane_block == table_ref[j, b]) & (lane_pos + j * block < len_ref[b])
                total = total + jnp.where(live, 1.0, 0.0)
            base[b : b + 1, :] = total
        row8 = lax.broadcasted_iota(jnp.int32, (BEAMS, BEAMS), 0)
        col8 = lax.broadcasted_iota(jnp.int32, (BEAMS, BEAMS), 1)
        new_row = lax.broadcasted_iota(jnp.int32, (BEAMS, LANES), 0)
        new_col = lax.broadcasted_iota(jnp.int32, (BEAMS, LANES), 1)
        state = jnp.concatenate([base[...], jnp.zeros((BEAMS, LANES), jnp.float32)], axis=1)
        found = []
        for s in range(steps):
            pick = jnp.zeros((BEAMS, BEAMS), jnp.float32)
            for b in range(BEAMS):
                pick = jnp.where((row8 == b) & (col8 == parents_ref[s, b]), 1.0, pick)
            state = jnp.dot(
                pick.astype(jnp.bfloat16), state.astype(jnp.bfloat16), preferred_element_type=jnp.float32
            )
            own = jnp.where(new_col == new_row + s * BEAMS, 1.0, 0.0)
            state = jnp.concatenate([state[:, :tokens], state[:, tokens:] + own], axis=1)
            found.append(state)
        found = jnp.concatenate(found, axis=0)
        return found[:, :tokens], found[:, tokens : tokens + rows]

    for copy in loads[:4]:
        copy.wait()
    meta_lane = lax.broadcasted_iota(jnp.int32, (16, LANES), 1)
    mark = (
        jnp.where(meta_lane < LANES // 2, place_ref[0], owned_ref[0])
        .astype(jnp.float32)
        .astype(jnp.bfloat16)
    )
    meta_c[o] = mark
    meta_p[p] = mark
    qa[o] = q_ref[:half, :]
    qb[p] = q_ref[half:, :]
    pl.semaphore_wait(barrier, outer - 1 + planes - 1 + len(tp_peers))
    first_hop(qa, column, qa_sem)
    first_hop(qb, plane, qb_sem)
    first_hop(meta_p, plane, meta_p_sem)
    first_hop(meta_c, column, meta_c_sem)
    loads[5].start()
    loads[6].start()
    loads[4].wait()
    split_blocks(prompt_raw, pk, pv)

    def marks_of(meta):
        rows_of = [meta[s].astype(jnp.float32) for s in range(meta.shape[0])]
        middle = LANES // 2
        return [r[0:1, 0:1] for r in rows_of], [r[0:1, middle : middle + 1] for r in rows_of]

    wait_hop(meta_p, plane, meta_p_sem)
    places_p, owners_p = marks_of(meta_p)
    wait_hop(qb, plane, qb_sem)
    second_hop(qb, places_p, qb_msg, qb_in, column, qb2_sem)
    wait_hop(meta_c, column, meta_c_sem)
    places_c, owners_c = marks_of(meta_c)
    wait_hop(qa, column, qa_sem)
    second_hop(qa, places_c, qa_msg, qa_in, plane, qa2_sem)
    for copy in loads[7:]:
        copy.start()
    loads[5].wait()
    loads[6].wait()
    split_blocks(home_raw, hk, hv)
    split_blocks(new_raw, nk, nv)
    wait_hop(qa_in, plane, qa2_sem)
    wait_hop(qb_in, column, qb2_sem)

    stat_lane = lax.broadcasted_iota(jnp.int32, (rows, LANES), 1)
    head_lane = stat_lane < heads

    def by_lane(values):
        packed = jnp.zeros((rows, LANES), jnp.float32)
        for h in range(heads):
            packed = jnp.where(stat_lane == h, values[h * rows : (h + 1) * rows], packed)
        return packed

    owned = owned_ref[0]
    asked = jnp.concatenate([qa_in[lax.rem(owned, planes)], qb_in[owned // planes]], axis=0)
    asked = spread_heads(asked, heads)
    scores = dot_t(asked, pk[...])
    prompt_lane = lax.broadcasted_iota(jnp.int32, scores.shape, 1)
    scores = jnp.where(prompt_lane < plen_ref[0], scores, NEG_FILL)
    top = jnp.max(scores, axis=1, keepdims=True)
    weights = jnp.exp(scores - top).astype(jnp.bfloat16)
    total = jnp.sum(weights.astype(jnp.float32), axis=1, keepdims=True)
    wide = jnp.dot(weights, pv[...], preferred_element_type=jnp.float32)
    total = by_lane(total)
    part_of = 1.0 / total
    rest = by_lane(top) + jnp.where(head_lane, jnp.log(total), 0.0)
    stats = jnp.zeros((rows, LANES), jnp.float32)
    for part in range(3):
        level = rest.astype(jnp.bfloat16).astype(jnp.float32)
        rest = rest - level
        stats = stats + (pltpu.roll(level, part * heads, 1) if part else level)

    def answer(h, cols):
        own = slice(h * rows, (h + 1) * rows)
        return wide[own, cols] * part_of[:, h : h + 1]

    answers = own_columns(rows, lanes, answer).astype(jnp.bfloat16)
    stats = stats.astype(jnp.bfloat16)
    ra[o, :, :lanes] = answers[:half]
    ra[o, :, lanes:] = stats[:half]
    rb[p, :, :lanes] = answers[half:]
    rb[p, :, lanes:] = stats[half:]
    first_hop(ra, column, ra_sem)
    first_hop(rb, plane, rb_sem)
    pool_count, new_count = key_counts()

    wait_hop(rb, plane, rb_sem)
    second_hop(rb, owners_p, rb_msg, rb_in, column, rb2_sem)
    query = spread_heads(q_ref[...], heads)
    pool_c = jnp.concatenate([pool_count] * heads, axis=0)
    new_c = jnp.concatenate([new_count] * heads, axis=0)
    pool_s = jnp.where(pool_c > 0.0, dot_t(query, hk[...]), NEG_FILL)
    new_s = jnp.where(new_c > 0.0, dot_t(query, nk[...]), NEG_FILL)
    home_top = jnp.maximum(
        jnp.max(pool_s, axis=1, keepdims=True), jnp.max(new_s, axis=1, keepdims=True)
    )
    pool_w = jnp.exp(pool_s - home_top).astype(jnp.bfloat16).astype(jnp.float32) * pool_c
    new_w = jnp.exp(new_s - home_top).astype(jnp.bfloat16)
    home_sum = jnp.sum(pool_w, axis=1, keepdims=True) + jnp.sum(
        new_w.astype(jnp.float32), axis=1, keepdims=True
    )
    numer = jnp.dot(pool_w.astype(jnp.bfloat16), hv[...], preferred_element_type=jnp.float32)
    numer = numer + jnp.dot(new_w, nv[...], preferred_element_type=jnp.float32)

    home_top = by_lane(home_top)
    home_sum = by_lane(home_sum)

    wait_hop(ra, column, ra_sem)
    second_hop(ra, owners_c, ra_msg, ra_in, plane, ra2_sem)
    wait_hop(ra_in, plane, ra2_sem)
    wait_hop(rb_in, column, rb2_sem)
    place = place_ref[0]
    reply = jnp.concatenate([ra_in[lax.rem(place, planes)], rb_in[place // planes]], axis=0)
    reply = reply.astype(jnp.float32)
    stats = reply[:, lanes:]
    reply_log = stats + pltpu.roll(stats, LANES - heads, 1) + pltpu.roll(stats, LANES - 2 * heads, 1)
    reply_log = jnp.where(head_lane, reply_log, 0.0)
    joint = jnp.maximum(home_top, reply_log)
    home_factor = jnp.exp(home_top - joint)
    prompt_factor = jnp.exp(reply_log - joint)
    scale = 1.0 / (home_sum * home_factor + prompt_factor)
    home_factor = home_factor * scale
    prompt_factor = prompt_factor * scale

    def joined(h, cols):
        own = slice(h * rows, (h + 1) * rows)
        lane = slice(h, h + 1)
        return numer[own, cols] * home_factor[:, lane] + reply[:, cols] * prompt_factor[:, lane]

    attended = own_columns(rows, lanes, joined).astype(jnp.bfloat16)

    loads[7].wait()
    for k in range(OUT_CHUNKS):
        cols = slice(k * chunk, (k + 1) * chunk)
        part = jnp.dot(attended, wo[:, cols], preferred_element_type=jnp.float32)
        obuf[my_tp, k] = part.astype(jnp.bfloat16)
        for d, peer in enumerate(tp_peers):
            mine = obuf.at[my_tp, k]
            push(mine, mine, osend.at[k * len(tp_peers) + d], orecv.at[my_tp, k], "tp", peer)

    for copy in loads[8:]:
        copy.wait()
    gain_all = gain_ref[...].astype(jnp.float32)
    square = jnp.zeros((rows, 1), jnp.float32)
    for k in range(OUT_CHUNKS):
        cols = slice(k * chunk, (k + 1) * chunk)
        for peer in tp_peers:
            arrive(obuf.at[peer, k], osend.at[0], orecv.at[peer, k], "tp", peer)
        summed = obuf[0, k].astype(jnp.float32)
        for t in range(1, tp_size):
            summed = summed + obuf[t, k].astype(jnp.float32)
        mixed = res_ref[:, cols].astype(jnp.float32) + summed
        res_out[:, cols] = mixed.astype(jnp.bfloat16)
        square = square + jnp.sum(mixed * mixed, axis=1, keepdims=True)
        gain_rows = [gain_all[n : n + 1] for n in range(k * chunk // LANES, (k + 1) * chunk // LANES)]
        gained = (mixed * jnp.concatenate(gain_rows, axis=1)).astype(jnp.bfloat16)
        for n in range(3):
            term = jnp.dot(gained, wq[n, cols, :], preferred_element_type=jnp.float32)
            if k == 0:
                acc[n] = term
            else:
                acc[n] += term
    inverse = lax.rsqrt(square / depth + NORM_EPS)
    for n in range(3):
        scaled = acc[n] * inverse
        for s in range(steps):
            qkv_out[s, n] = scaled[s * BEAMS : (s + 1) * BEAMS].astype(jnp.bfloat16)

    for copy in sent:
        copy.wait_send()


def token_rows(cache):
    lanes = cache.shape[-1]
    tiles = cache.reshape(-1, 2, lanes // LANES, LANES).transpose(0, 2, 1, 3)
    return tiles.reshape(-1, LANES)


def shards(
    queries, new_kv, residual, home_cache, prompt_cache, home_table, home_len,
    parents, prompt_place, owned_request, prompt_len, out_weight, norm_gain, qkv_weight,
):
    steps, beams, lanes = queries.shape
    rows = steps * beams
    depth = residual.shape[2]
    req_size = lax.axis_size("req")
    tp_size = lax.axis_size("tp")
    outer, inner = grid_of(req_size)
    planes = 2 * inner
    tokens = home_cache.shape[0] * home_cache.shape[1]
    smem = pl.BlockSpec(memory_space=pltpu.SMEM)
    vmem = pl.BlockSpec(memory_space=pltpu.VMEM)
    hbm = pl.BlockSpec(memory_space=pltpu.HBM)
    bf16, f32 = jnp.bfloat16, jnp.float32
    dma = pltpu.SemaphoreType.DMA
    singles = (prompt_place, owned_request, prompt_len)
    ints = (home_table.T, home_len, parents)
    floats = (
        queries.reshape(rows, lanes),
        token_rows(new_kv),
        residual.reshape(rows, depth),
        norm_gain.reshape(-1, LANES),
        token_rows(home_cache),
        token_rows(prompt_cache),
        out_weight,
        qkv_weight.transpose(1, 0, 2),
    )
    wide = lanes + LANES
    half = rows // 2

    def route(first, second, width):
        return [
            pltpu.VMEM((first, half, width), bf16),
            pltpu.VMEM((second - 1, half, width), bf16),
            pltpu.VMEM((second, half, width), bf16),
        ]

    hops = [outer, planes] + [outer, planes, planes, outer] * 2
    sems = [(len(ints) + len(floats),), (OUT_CHUNKS * tp_size,), (tp_size, OUT_CHUNKS)]
    sems += [(size,) for size in hops for _ in range(2)]
    qkv, res = pl.pallas_call(
        functools.partial(kernel, req_size, tp_size, steps),
        out_shape=(
            jax.ShapeDtypeStruct((steps, 3, beams, lanes), bf16),
            jax.ShapeDtypeStruct((rows, depth), bf16),
        ),
        in_specs=[smem] * len(singles) + [hbm] * (len(ints) + len(floats)),
        out_specs=(vmem, vmem),
        scratch_shapes=[pltpu.SMEM(a.shape, jnp.int32) for a in ints]
        + [pltpu.VMEM(a.shape, bf16) for a in floats]
        + [
            pltpu.VMEM((outer, 16, LANES), bf16),
            pltpu.VMEM((planes, 16, LANES), bf16),
        ]
        + route(outer, planes, lanes)
        + route(planes, outer, lanes)
        + route(outer, planes, wide)
        + route(planes, outer, wide)
        + [
            pltpu.VMEM((tp_size, OUT_CHUNKS, rows, depth // OUT_CHUNKS), bf16),
            pltpu.VMEM((rows, lanes), bf16),
            pltpu.VMEM((rows, lanes), bf16),
            pltpu.VMEM((tokens, lanes), bf16),
            pltpu.VMEM((tokens, lanes), bf16),
            pltpu.VMEM((tokens, lanes), bf16),
            pltpu.VMEM((tokens, lanes), bf16),
            pltpu.VMEM((beams, tokens), f32),
            pltpu.VMEM((3, rows, lanes), f32),
        ]
        + [dma(shape) for shape in sems],
        compiler_params=pltpu.CompilerParams(
            collective_id=0, has_side_effects=True, vmem_limit_bytes=40 * 1024 * 1024
        ),
    )(*singles, *(pltpu.with_memory_space_constraint(x, pltpu.HBM) for x in ints + floats))
    return qkv.transpose(0, 2, 1, 3), res.reshape(steps, beams, depth)


def solution(mesh):
    placed = (
        P(None, "req", "tp"),
        P(None, "req", None, "tp"),
        P(None, "req", None),
        P("req", None, None, "tp"),
        P("req", None, None, "tp"),
        P("req", None),
        P("req"),
        P(None, "req"),
        P("req"),
        P("req"),
        P("req"),
        P("tp", None),
        P(),
        P(None, None, "tp"),
    )
    return jax.shard_map(
        shards,
        mesh=mesh,
        in_specs=placed,
        out_specs=(P(None, "req", None, "tp"), P(None, "req", None)),
        check_vma=False,
    )
```

```python
import functools
import math

import jax
import jax.numpy as jnp
from jax import lax
from jax.experimental import pallas as pl
from jax.experimental.pallas import tpu as pltpu
from jax.sharding import PartitionSpec as P

HEAD_DIM = 64
BEAMS = 8
LANES = 128
OUT_CHUNKS = 8
SPLIT = 32

NEG_FILL = -1e30
NORM_EPS = 1e-05


def grid_of(req_size):
    chips = req_size // 2
    outer = 4 if chips % 4 == 0 else 1
    return outer, chips // outer


def spread_heads(q, heads):
    rows, lanes = q.shape
    scaled = q.astype(jnp.float32) * (1.0 / math.sqrt(HEAD_DIM))
    lane_head = lax.broadcasted_iota(jnp.int32, (rows, lanes), 1) // HEAD_DIM
    parts = [jnp.where(lane_head == h, scaled, 0.0) for h in range(heads)]
    return jnp.concatenate(parts, axis=0).astype(jnp.bfloat16)


def dot_t(a, b):
    return lax.dot_general(a, b, (((1,), (1,)), ((), ())), preferred_element_type=jnp.float32)


def own_columns(rows, lanes, piece):
    first = lax.broadcasted_iota(jnp.int32, (rows, LANES), 1) < HEAD_DIM
    tiles = []
    for t in range(lanes // LANES):
        cols = slice(t * LANES, (t + 1) * LANES)
        tiles.append(jnp.where(first, piece(2 * t, cols), piece(2 * t + 1, cols)))
    return tiles[0] if len(tiles) == 1 else jnp.concatenate(tiles, axis=1)


def split_blocks(raw, keys, values):
    tokens, lanes = keys.shape
    kinds = 2 * (lanes // LANES)
    size = SPLIT * kinds
    out_row = lax.broadcasted_iota(jnp.int32, (size, size), 0)
    in_row = lax.broadcasted_iota(jnp.int32, (size, size), 1)
    wanted = (out_row % SPLIT) * kinds + out_row // SPLIT
    order = jnp.where(in_row == wanted, 1.0, 0.0).astype(jnp.bfloat16)
    blocks = tokens // SPLIT
    group = min(4, blocks)
    for first in range(0, blocks, group):
        taken = range(first, first + group)
        beside = [raw[n * size : (n + 1) * size, :] for n in taken]
        beside = beside[0] if group == 1 else jnp.concatenate(beside, axis=1)
        ordered = jnp.dot(order, beside, preferred_element_type=jnp.float32).astype(jnp.bfloat16)
        for g, n in enumerate(taken):
            rows, own = slice(n * SPLIT, (n + 1) * SPLIT), slice(g * LANES, (g + 1) * LANES)
            for t in range(lanes // LANES):
                at = 2 * t * SPLIT
                cols = slice(t * LANES, (t + 1) * LANES)
                keys[rows, cols] = ordered[at : at + SPLIT, own]
                values[rows, cols] = ordered[at + SPLIT : at + 2 * SPLIT, own]


def kernel(
    req_size, tp_size, steps,
    place_ref, owned_ref, plen_ref, table_any, len_any, parents_any,
    q_any, new_any, res_any, gain_any, home_any, prompt_any, wo_any, wq_any,
    qkv_out, res_out,
    table_ref, len_ref, parents_ref,
    q_ref, new_raw, res_ref, gain_ref, home_raw, prompt_raw, wo, wq,
    meta_c, meta_p, qa, qa_msg, qa_in, qb, qb_msg, qb_in, ra, ra_msg, ra_in, rb, rb_msg, rb_in, obuf,
    nk, nv, hk, hv, pk, pv, base, acc,
    load_sem, osend, orecv, *hop_sems
):
    rows, lanes = q_ref.shape
    heads = lanes // HEAD_DIM
    depth = res_ref.shape[1]
    chunk = depth // OUT_CHUNKS
    tokens = hk.shape[0]
    block_count = table_ref.shape[0]
    block = tokens // block_count
    outer, inner = grid_of(req_size)
    planes = 2 * inner
    me = lax.axis_index("req")
    my_tp = lax.axis_index("tp")
    o = me // planes
    p = lax.rem(me, planes)

    half = rows // 2
    mesh_id = pl.DeviceIdType.MESH
    column = (outer, o, lambda n: n * planes + p)
    plane = (planes, p, lambda n: o * planes + n)

    def others(group):
        size, mine, _ = group
        return [lax.rem(mine + d, size) for d in range(1, size)]

    sem_pairs = [hop_sems[n : n + 2] for n in range(0, len(hop_sems), 2)]
    meta_c_sem, meta_p_sem, qa_sem, qa2_sem, qb_sem, qb2_sem, ra_sem, ra2_sem, rb_sem, rb2_sem = sem_pairs
    tp_peers = [lax.rem(my_tp + d, tp_size) for d in range(1, tp_size)]

    barrier = pltpu.get_barrier_semaphore()
    for group in (column, plane):
        for n in others(group):
            pl.semaphore_signal(barrier, inc=1, device_id={"req": group[2](n)}, device_id_type=mesh_id)
    for peer in tp_peers:
        pl.semaphore_signal(barrier, inc=1, device_id={"tp": peer}, device_id_type=mesh_id)

    pairs = [
        (q_any, q_ref), (table_any, table_ref), (len_any, len_ref), (parents_any, parents_ref),
        (prompt_any, prompt_raw), (home_any, home_raw), (new_any, new_raw),
        (wo_any, wo), (res_any, res_ref), (gain_any, gain_ref), (wq_any, wq),
    ]
    loads = [pltpu.make_async_copy(src, dst, load_sem.at[n]) for n, (src, dst) in enumerate(pairs)]
    for copy in loads[:5]:
        copy.start()
    sent = []

    def push(src, dst, send_sem, recv_sem, axis, peer):
        copy = pltpu.make_async_remote_copy(
            src_ref=src, dst_ref=dst, send_sem=send_sem, recv_sem=recv_sem,
            device_id={axis: peer}, device_id_type=mesh_id,
        )
        copy.start()
        sent.append(copy)

    def arrive(dst, send_sem, recv_sem, axis, peer):
        pltpu.make_async_remote_copy(
            src_ref=dst, dst_ref=dst, send_sem=send_sem, recv_sem=recv_sem,
            device_id={axis: peer}, device_id_type=mesh_id,
        ).wait_recv()

    def first_hop(buf, group, sems):
        _, mine, index = group
        for d, n in enumerate(others(group)):
            push(buf.at[mine], buf.at[mine], sems[0].at[d], sems[1].at[mine], "req", index(n))

    def wait_hop(buf, group, sems):
        for n in others(group):
            arrive(buf.at[n], sems[0].at[0], sems[1].at[n], "req", group[2](n))

    def second_hop(buf, marks, msg, landed, group, sems):
        held = [buf[s].astype(jnp.float32) for s in range(buf.shape[0])]
        _, mine, index = group

        def chosen(target):
            value = held[0]
            for s in range(1, len(held)):
                value = jnp.where(marks[s] == target.astype(jnp.float32), held[s], value)
            return value.astype(jnp.bfloat16)

        for d, n in enumerate(others(group)):
            msg[d] = chosen(index(n))
            push(msg.at[d], landed.at[mine], sems[0].at[d], sems[1].at[mine], "req", index(n))
        landed[mine] = chosen(me)

    def key_counts():
        lane = lax.broadcasted_iota(jnp.int32, (1, tokens), 1)
        lane_block = lane // block
        lane_pos = lane - lane_block * block
        for b in range(BEAMS):
            total = jnp.zeros((1, tokens), jnp.float32)
            for j in range(block_count):
                live = (lane_block == table_ref[j, b]) & (lane_pos + j * block < len_ref[b])
                total = total + jnp.where(live, 1.0, 0.0)
            base[b : b + 1, :] = total
        row8 = lax.broadcasted_iota(jnp.int32, (BEAMS, BEAMS), 0)
        col8 = lax.broadcasted_iota(jnp.int32, (BEAMS, BEAMS), 1)
        new_row = lax.broadcasted_iota(jnp.int32, (BEAMS, LANES), 0)
        new_col = lax.broadcasted_iota(jnp.int32, (BEAMS, LANES), 1)
        state = jnp.concatenate([base[...], jnp.zeros((BEAMS, LANES), jnp.float32)], axis=1)
        found = []
        for s in range(steps):
            pick = jnp.zeros((BEAMS, BEAMS), jnp.float32)
            for b in range(BEAMS):
                pick = jnp.where((row8 == b) & (col8 == parents_ref[s, b]), 1.0, pick)
            state = jnp.dot(
                pick.astype(jnp.bfloat16), state.astype(jnp.bfloat16), preferred_element_type=jnp.float32
            )
            own = jnp.where(new_col == new_row + s * BEAMS, 1.0, 0.0)
            state = jnp.concatenate([state[:, :tokens], state[:, tokens:] + own], axis=1)
            found.append(state)
        found = jnp.concatenate(found, axis=0)
        return found[:, :tokens], found[:, tokens : tokens + rows]

    for copy in loads[:4]:
        copy.wait()
    meta_lane = lax.broadcasted_iota(jnp.int32, (16, LANES), 1)
    mark = (
        jnp.where(meta_lane < LANES // 2, place_ref[0], owned_ref[0])
        .astype(jnp.float32)
        .astype(jnp.bfloat16)
    )
    meta_c[o] = mark
    meta_p[p] = mark
    qa[o] = q_ref[:half, :]
    qb[p] = q_ref[half:, :]
    pl.semaphore_wait(barrier, outer - 1 + planes - 1 + len(tp_peers))
    first_hop(qa, column, qa_sem)
    first_hop(qb, plane, qb_sem)
    first_hop(meta_p, plane, meta_p_sem)
    first_hop(meta_c, column, meta_c_sem)
    loads[5].start()
    loads[6].start()
    loads[4].wait()
    split_blocks(prompt_raw, pk, pv)

    def marks_of(meta):
        rows_of = [meta[s].astype(jnp.float32) for s in range(meta.shape[0])]
        middle = LANES // 2
        return [r[0:1, 0:1] for r in rows_of], [r[0:1, middle : middle + 1] for r in rows_of]

    wait_hop(meta_p, plane, meta_p_sem)
    places_p, owners_p = marks_of(meta_p)
    wait_hop(qb, plane, qb_sem)
    second_hop(qb, places_p, qb_msg, qb_in, column, qb2_sem)
    wait_hop(meta_c, column, meta_c_sem)
    places_c, owners_c = marks_of(meta_c)
    wait_hop(qa, column, qa_sem)
    second_hop(qa, places_c, qa_msg, qa_in, plane, qa2_sem)
    for copy in loads[7:]:
        copy.start()
    loads[5].wait()
    loads[6].wait()
    split_blocks(home_raw, hk, hv)
    split_blocks(new_raw, nk, nv)
    wait_hop(qa_in, plane, qa2_sem)
    wait_hop(qb_in, column, qb2_sem)

    stat_lane = lax.broadcasted_iota(jnp.int32, (rows, LANES), 1)
    head_lane = stat_lane < heads

    def by_lane(values):
        packed = jnp.zeros((rows, LANES), jnp.float32)
        for h in range(heads):
            packed = jnp.where(stat_lane == h, values[h * rows : (h + 1) * rows], packed)
        return packed

    owned = owned_ref[0]
    asked = jnp.concatenate([qa_in[lax.rem(owned, planes)], qb_in[owned // planes]], axis=0)
    asked = spread_heads(asked, heads)
    scores = dot_t(asked, pk[...])
    prompt_lane = lax.broadcasted_iota(jnp.int32, scores.shape, 1)
    scores = jnp.where(prompt_lane < plen_ref[0], scores, NEG_FILL)
    top = jnp.max(scores, axis=1, keepdims=True)
    weights = jnp.exp(scores - top).astype(jnp.bfloat16)
    total = jnp.sum(weights.astype(jnp.float32), axis=1, keepdims=True)
    wide = jnp.dot(weights, pv[...], preferred_element_type=jnp.float32)
    total = by_lane(total)
    part_of = 1.0 / total
    rest = by_lane(top) + jnp.where(head_lane, jnp.log(total), 0.0)
    stats = jnp.zeros((rows, LANES), jnp.float32)
    for part in range(3):
        level = rest.astype(jnp.bfloat16).astype(jnp.float32)
        rest = rest - level
        stats = stats + (pltpu.roll(level, part * heads, 1) if part else level)

    def answer(h, cols):
        own = slice(h * rows, (h + 1) * rows)
        return wide[own, cols] * part_of[:, h : h + 1]

    answers = own_columns(rows, lanes, answer).astype(jnp.bfloat16)
    stats = stats.astype(jnp.bfloat16)
    ra[o, :, :lanes] = answers[:half]
    ra[o, :, lanes:] = stats[:half]
    rb[p, :, :lanes] = answers[half:]
    rb[p, :, lanes:] = stats[half:]
    first_hop(ra, column, ra_sem)
    first_hop(rb, plane, rb_sem)
    pool_count, new_count = key_counts()

    wait_hop(rb, plane, rb_sem)
    second_hop(rb, owners_p, rb_msg, rb_in, column, rb2_sem)
    query = spread_heads(q_ref[...], heads)
    pool_c = jnp.concatenate([pool_count] * heads, axis=0)
    new_c = jnp.concatenate([new_count] * heads, axis=0)
    pool_s = jnp.where(pool_c > 0.0, dot_t(query, hk[...]), NEG_FILL)
    new_s = jnp.where(new_c > 0.0, dot_t(query, nk[...]), NEG_FILL)
    home_top = jnp.maximum(
        jnp.max(pool_s, axis=1, keepdims=True), jnp.max(new_s, axis=1, keepdims=True)
    )
    pool_w = jnp.exp(pool_s - home_top).astype(jnp.bfloat16).astype(jnp.float32) * pool_c
    new_w = jnp.exp(new_s - home_top).astype(jnp.bfloat16)
    home_sum = jnp.sum(pool_w, axis=1, keepdims=True) + jnp.sum(
        new_w.astype(jnp.float32), axis=1, keepdims=True
    )
    numer = jnp.dot(pool_w.astype(jnp.bfloat16), hv[...], preferred_element_type=jnp.float32)
    numer = numer + jnp.dot(new_w, nv[...], preferred_element_type=jnp.float32)

    home_top = by_lane(home_top)
    home_sum = by_lane(home_sum)

    wait_hop(ra, column, ra_sem)
    second_hop(ra, owners_c, ra_msg, ra_in, plane, ra2_sem)
    wait_hop(ra_in, plane, ra2_sem)
    wait_hop(rb_in, column, rb2_sem)
    place = place_ref[0]
    reply = jnp.concatenate([ra_in[lax.rem(place, planes)], rb_in[place // planes]], axis=0)
    reply = reply.astype(jnp.float32)
    stats = reply[:, lanes:]
    reply_log = stats + pltpu.roll(stats, LANES - heads, 1) + pltpu.roll(stats, LANES - 2 * heads, 1)
    reply_log = jnp.where(head_lane, reply_log, 0.0)
    joint = jnp.maximum(home_top, reply_log)
    home_factor = jnp.exp(home_top - joint)
    prompt_factor = jnp.exp(reply_log - joint)
    scale = 1.0 / (home_sum * home_factor + prompt_factor)
    home_factor = home_factor * scale
    prompt_factor = prompt_factor * scale

    def joined(h, cols):
        own = slice(h * rows, (h + 1) * rows)
        lane = slice(h, h + 1)
        return numer[own, cols] * home_factor[:, lane] + reply[:, cols] * prompt_factor[:, lane]

    attended = own_columns(rows, lanes, joined).astype(jnp.bfloat16)

    loads[7].wait()
    for k in range(OUT_CHUNKS):
        cols = slice(k * chunk, (k + 1) * chunk)
        part = jnp.dot(attended, wo[:, cols], preferred_element_type=jnp.float32)
        obuf[my_tp, k] = part.astype(jnp.bfloat16)
        for d, peer in enumerate(tp_peers):
            mine = obuf.at[my_tp, k]
            push(mine, mine, osend.at[k * len(tp_peers) + d], orecv.at[my_tp, k], "tp", peer)

    for copy in loads[8:]:
        copy.wait()
    gain_all = gain_ref[...].astype(jnp.float32)
    square = jnp.zeros((rows, 1), jnp.float32)
    for k in range(OUT_CHUNKS):
        cols = slice(k * chunk, (k + 1) * chunk)
        for peer in tp_peers:
            arrive(obuf.at[peer, k], osend.at[0], orecv.at[peer, k], "tp", peer)
        summed = obuf[0, k].astype(jnp.float32)
        for t in range(1, tp_size):
            summed = summed + obuf[t, k].astype(jnp.float32)
        mixed = res_ref[:, cols].astype(jnp.float32) + summed
        res_out[:, cols] = mixed.astype(jnp.bfloat16)
        square = square + jnp.sum(mixed * mixed, axis=1, keepdims=True)
        gain_rows = [gain_all[n : n + 1] for n in range(k * chunk // LANES, (k + 1) * chunk // LANES)]
        gained = (mixed * jnp.concatenate(gain_rows, axis=1)).astype(jnp.bfloat16)
        for n in range(3):
            term = jnp.dot(gained, wq[n, cols, :], preferred_element_type=jnp.float32)
            if k == 0:
                acc[n] = term
            else:
                acc[n] += term
    inverse = lax.rsqrt(square / depth + NORM_EPS)
    for n in range(3):
        scaled = acc[n] * inverse
        for s in range(steps):
            qkv_out[s, n] = scaled[s * BEAMS : (s + 1) * BEAMS].astype(jnp.bfloat16)

    for copy in sent:
        copy.wait_send()


def token_rows(cache):
    lanes = cache.shape[-1]
    tiles = cache.reshape(-1, 2, lanes // LANES, LANES).transpose(0, 2, 1, 3)
    return tiles.reshape(-1, LANES)


def shards(
    queries, new_kv, residual, home_cache, prompt_cache, home_table, home_len,
    parents, prompt_place, owned_request, prompt_len, out_weight, norm_gain, qkv_weight,
):
    steps, beams, lanes = queries.shape
    rows = steps * beams
    depth = residual.shape[2]
    req_size = lax.axis_size("req")
    tp_size = lax.axis_size("tp")
    outer, inner = grid_of(req_size)
    planes = 2 * inner
    tokens = home_cache.shape[0] * home_cache.shape[1]
    smem = pl.BlockSpec(memory_space=pltpu.SMEM)
    vmem = pl.BlockSpec(memory_space=pltpu.VMEM)
    hbm = pl.BlockSpec(memory_space=pltpu.HBM)
    bf16, f32 = jnp.bfloat16, jnp.float32
    dma = pltpu.SemaphoreType.DMA
    singles = (prompt_place, owned_request, prompt_len)
    ints = (home_table.T, home_len, parents)
    floats = (
        queries.reshape(rows, lanes),
        token_rows(new_kv),
        residual.reshape(rows, depth),
        norm_gain.reshape(-1, LANES),
        token_rows(home_cache),
        token_rows(prompt_cache),
        out_weight,
        qkv_weight.transpose(1, 0, 2),
    )
    wide = lanes + LANES
    half = rows // 2

    def route(first, second, width):
        return [
            pltpu.VMEM((first, half, width), bf16),
            pltpu.VMEM((second - 1, half, width), bf16),
            pltpu.VMEM((second, half, width), bf16),
        ]

    hops = [outer, planes] + [outer, planes, planes, outer] * 2
    sems = [(len(ints) + len(floats),), (OUT_CHUNKS * tp_size,), (tp_size, OUT_CHUNKS)]
    sems += [(size,) for size in hops for _ in range(2)]
    qkv, res = pl.pallas_call(
        functools.partial(kernel, req_size, tp_size, steps),
        out_shape=(
            jax.ShapeDtypeStruct((steps, 3, beams, lanes), bf16),
            jax.ShapeDtypeStruct((rows, depth), bf16),
        ),
        in_specs=[smem] * len(singles) + [hbm] * (len(ints) + len(floats)),
        out_specs=(vmem, vmem),
        scratch_shapes=[pltpu.SMEM(a.shape, jnp.int32) for a in ints]
        + [pltpu.VMEM(a.shape, bf16) for a in floats]
        + [
            pltpu.VMEM((outer, 16, LANES), bf16),
            pltpu.VMEM((planes, 16, LANES), bf16),
        ]
        + route(outer, planes, lanes)
        + route(planes, outer, lanes)
        + route(outer, planes, wide)
        + route(planes, outer, wide)
        + [
            pltpu.VMEM((tp_size, OUT_CHUNKS, rows, depth // OUT_CHUNKS), bf16),
            pltpu.VMEM((rows, lanes), bf16),
            pltpu.VMEM((rows, lanes), bf16),
            pltpu.VMEM((tokens, lanes), bf16),
            pltpu.VMEM((tokens, lanes), bf16),
            pltpu.VMEM((tokens, lanes), bf16),
            pltpu.VMEM((tokens, lanes), bf16),
            pltpu.VMEM((beams, tokens), f32),
            pltpu.VMEM((3, rows, lanes), f32),
        ]
        + [dma(shape) for shape in sems],
        compiler_params=pltpu.CompilerParams(
            collective_id=0, has_side_effects=True, vmem_limit_bytes=40 * 1024 * 1024
        ),
    )(*singles, *(pltpu.with_memory_space_constraint(x, pltpu.HBM) for x in ints + floats))
    return qkv.transpose(0, 2, 1, 3), res.reshape(steps, beams, depth)


def solution(mesh):
    placed = (
        P(None, "req", "tp"),
        P(None, "req", None, "tp"),
        P(None, "req", None),
        P("req", None, None, "tp"),
        P("req", None, None, "tp"),
        P("req", None),
        P("req"),
        P(None, "req"),
        P("req"),
        P("req"),
        P("req"),
        P("tp", None),
        P(),
        P(None, None, "tp"),
    )
    return jax.shard_map(
        shards,
        mesh=mesh,
        in_specs=placed,
        out_specs=(P(None, "req", None, "tp"), P(None, "req", None)),
        check_vma=False,
    )
```
